256 devices in a mesh: lang: 8 (over z), shard: 32 (over y, x, core).
Axes of the slice: x: 4, y: 4, z: 8, core: 2. Of those that a mesh axis runs over, the one named last changes fastest.
Arguments:
- memory: bfloat16 [256, 16, 4096], P(('lang', 'shard')), may hold values from -6 to 6
- lang_id: int32 [256], P(('lang', 'shard')), may hold values from 0 to 7, as said below
- src_len: int32 [256], P(('lang', 'shard')), may hold values from 4 to 16
- tgt_len: int32 [256], P(('lang', 'shard')), may hold values from 32 to 128
- queries: bfloat16 [8, 64, 128, 4096], P('lang', 'shard'), may hold values from -64 to 64
- key_weight: bfloat16 [8, 4096, 4096], P('lang', None, 'shard'), may hold values from -1 to 1
- value_weight: bfloat16 [8, 4096, 4096], P('lang', None, 'shard'), may hold values from -0.09375 to 0.09375
- grad_context: bfloat16 [8, 64, 128, 4096], P('lang', 'shard'), may hold values from -6 to 6
Outputs:
- context: bfloat16 [8, 64, 128, 4096], P('lang', 'shard')
- grad_queries: bfloat16 [8, 64, 128, 4096], P('lang', 'shard')
- grad_memory: bfloat16 [256, 16, 4096], P(('lang', 'shard'))
- grad_key_weight: bfloat16 [8, 4096, 4096], P('lang', None, 'shard')
- grad_value_weight: bfloat16 [8, 4096, 4096], P('lang', None, 'shard')
The draws below stay inside these ranges and needn't reach their ends.
Inputs may be any that keep to these rules, and one draw needn't show every extreme that they name: `lang_id`: among the 8 sentences of one column b (indices a * 32 + b), no language is named more than 2 times, and in every column some language is named exactly 2 times.
All inputs are finite; a program needn't handle non-finite values.
Results may differ from the reference program's by a relative error of at most 0.025.
The reference program's roundings to bfloat16 on the way count: a program that leaves them out, or rounds other values in their place, can miss the bound.
Values may be sent and summed in bfloat16 or wider, within the bound.
No kernel may reach another device: no remote copies, remote signals or barrier semaphores. Data moves between devices by JAX's collectives and lax.ppermute only.
A program may use at most 128 MiB of HBM per device.

```python
import jax
import jax.numpy as jnp
from jax import lax

D = 4096
HEADS = 32
HEAD = 128
LT = 128
LS = 16
MOST = 2
HK = 4096
LANGS = 8
SLOTS = 64
SENTS = 256
N_SHARD = 32


def draw_lang_id(key, part):
    key = jax.random.fold_in(key, 11)
    columns = SENTS // LANGS
    key_favour, key_first, key_second, key_sets, key_order = jax.random.split(key, 5)
    favoured = jax.random.permutation(key_favour, LANGS)
    first_pick = jax.random.randint(key_first, (columns,), 0, LANGS)
    second_pick = jax.random.randint(key_second, (columns,), 0, LANGS)
    pair_lang = favoured[jnp.minimum(first_pick, second_pick)]

    def shuffle_doubled(row_key):
        return jax.random.permutation(row_key, 2 * LANGS)

    def shuffle_column(row_key):
        return jax.random.permutation(row_key, LANGS)
    shuffles = jax.vmap(shuffle_doubled)(jax.random.split(key_sets, columns))
    language = shuffles // 2
    ordering = jnp.argsort(shuffles + jnp.where(language == pair_lang[:, None], 2 * LANGS, 0), axis=1, stable=True)
    chosen = jnp.take_along_axis(language, ordering, axis=1)[:, :LANGS - 2]
    column_ids = jnp.concatenate([pair_lang[:, None], pair_lang[:, None], chosen], axis=1)
    placing = jax.vmap(shuffle_column)(jax.random.split(key_order, columns))
    column_ids = jnp.take_along_axis(column_ids, placing, axis=1)
    return column_ids.T.reshape(SENTS).astype(jnp.int32)


def draw_src_len(key, part):
    key = jax.random.fold_in(key, 12)
    lengths = jax.random.randint(key, (SENTS,), max(1, LS // 4), LS + 1)
    return lengths.at[0].set(LS).astype(jnp.int32)


def draw_tgt_len(key, part):
    key = jax.random.fold_in(key, 13)
    lengths = jax.random.randint(key, (SENTS,), max(1, LT // 4), LT + 1)
    return lengths.at[0].set(LT).astype(jnp.int32)


def draw_queries(key, part):
    key = jax.random.fold_in(key, 14)
    key_base = jax.random.fold_in(key, 0)
    values = jax.random.truncated_normal(key_base, -4.0, 4.0, (LANGS, SLOTS, LT, HK), jnp.float32)
    return values.astype(jnp.bfloat16)


def draw_memory(key, part):
    key = jax.random.fold_in(key, 15)
    values = jax.random.truncated_normal(key, -6.0, 6.0, (SENTS, LS, D), jnp.float32)
    return values.astype(jnp.bfloat16)


def draw_key_weight(key, part):
    key = jax.random.fold_in(key, 16)
    weights = jax.random.truncated_normal(key, -4.0, 4.0, (LANGS, D, HK), jnp.float32) * D ** (-0.5)
    return weights.astype(jnp.bfloat16)


def level_of(stream_key, dims, pieces, low, top_value):
    factor_of = 1.0
    for dim, shards_of in pieces:
        draws = jax.random.uniform(jax.random.fold_in(jax.random.fold_in(stream_key, 6), dim), (shards_of,), jnp.float32, low / len(pieces), top_value / len(pieces))
        factor_of = factor_of * jnp.repeat(jnp.exp(draws), dims[dim] // shards_of).reshape((-1,) + (1,) * (len(dims) - 1 - dim))
    return factor_of


def normal_values(own_key, extent, width, limit, cuts=(), held_as=jnp.bfloat16):
    result = jax.random.normal(own_key, extent, jnp.float32) * width
    if len(cuts) > 0:
        result = level_of(own_key, extent, cuts, -0.22, 0.18) * result
    return jnp.clip(result, min=-limit, max=limit).astype(held_as)


def setup_inputs(seed: int = 0) -> dict:
    seeds = jax.random.split(jax.random.key(seed), 9)
    memory = draw_memory(jax.random.fold_in(seeds[8], 71), 0)
    lang_id = draw_lang_id(jax.random.fold_in(seeds[8], 71), 0)
    src_len = draw_src_len(jax.random.fold_in(seeds[8], 71), 0)
    tgt_len = draw_tgt_len(jax.random.fold_in(seeds[8], 71), 0)
    queries = draw_queries(jax.random.fold_in(seeds[8], 71), 0)
    key_weight = draw_key_weight(jax.random.fold_in(seeds[8], 71), 0)
    value_weight = normal_values(seeds[6], (LANGS, D, HK), D ** -0.5, 0.09375, ((0, 8), (2, 32)))
    grad_context = normal_values(seeds[7], (LANGS, SLOTS, LT, HK), 1.0, 6.0, ((0, 8), (1, 32)))
    return dict(memory=memory, lang_id=lang_id, src_len=src_len, tgt_len=tgt_len, queries=queries, key_weight=key_weight, value_weight=value_weight, grad_context=grad_context)


masked_score = -1e30


def route_slots(lang_id):
    columns = SENTS // LANGS
    grid = lang_id.reshape(LANGS, columns)
    matching = grid[:, None, :] == grid[None, :, :]
    earlier = jnp.arange(LANGS)[None, :] < jnp.arange(LANGS)[:, None]
    position = jnp.sum(jnp.where(matching & earlier[:, :, None], 1, 0), axis=1).astype(jnp.int32)
    slot = jnp.arange(columns, dtype=jnp.int32)[None, :] * MOST + position
    return slot.reshape(SENTS).astype(jnp.int32)


def attend(queries, key_rows, value_rows, grad_ctx, src_slot, tgt_slot):
    scaling = HEAD ** -0.5
    query_f = queries.astype(jnp.float32)
    key_f = key_rows.astype(jnp.float32)
    value_f = value_rows.astype(jnp.float32)
    scores = jnp.einsum("nqhe,nkhe->nhqk", query_f, key_f) * scaling
    key_valid = jnp.arange(LS)[None, :] < jnp.maximum(src_slot, 1)[:, None]
    scores = jnp.where(key_valid[:, None, None, :], scores, masked_score)
    row_max = jnp.max(scores, axis=-1, keepdims=True)
    shifted = jnp.exp(scores - row_max)
    attention = shifted / jnp.sum(shifted, axis=-1, keepdims=True)
    attention_bf = attention.astype(jnp.bfloat16).astype(jnp.float32)
    row_valid = (jnp.arange(LT)[None, :] < tgt_slot[:, None])[:, :, None, None]
    context = jnp.einsum("nhqk,nkhe->nqhe", attention_bf, value_f)
    context = jnp.where(row_valid, context, 0.0).astype(jnp.bfloat16)
    grad_masked = jnp.where(row_valid, grad_ctx.astype(jnp.float32), 0.0)
    grad_values = jnp.einsum("nhqk,nqhe->nkhe", attention_bf, grad_masked).astype(jnp.bfloat16)
    grad_attention = jnp.einsum("nqhe,nkhe->nhqk", grad_masked, value_f)
    row_dot = jnp.sum(attention * grad_attention, axis=-1, keepdims=True)
    grad_scores = (attention * (grad_attention - row_dot)).astype(jnp.bfloat16).astype(jnp.float32)
    grad_queries = (jnp.einsum("nhqk,nkhe->nqhe", grad_scores, key_f) * scaling).astype(jnp.bfloat16)
    grad_keys = (jnp.einsum("nhqk,nqhe->nkhe", grad_scores, query_f) * scaling).astype(jnp.bfloat16)
    return context, grad_queries, grad_keys, grad_values


def one_language(inputs):
    routed, src_slot, tgt_slot, queries, key_weight, value_weight, grad_context = inputs
    flattened = routed.reshape(SLOTS * LS, D)
    key_rows = jnp.dot(flattened, key_weight, preferred_element_type=jnp.float32).astype(jnp.bfloat16)
    value_rows = jnp.dot(flattened, value_weight, preferred_element_type=jnp.float32).astype(jnp.bfloat16)
    source_shape = (SLOTS, LS, HEADS, HEAD)
    target_shape = (SLOTS, LT, HEADS, HEAD)
    context, grad_queries, grad_keys, grad_values = attend(
        queries.reshape(target_shape), key_rows.reshape(source_shape), value_rows.reshape(source_shape),
        grad_context.reshape(target_shape), src_slot, tgt_slot)
    grad_keys = grad_keys.reshape(SLOTS * LS, HK)
    grad_values = grad_values.reshape(SLOTS * LS, HK)
    grad_key_weight = jnp.dot(flattened.T, grad_keys, preferred_element_type=jnp.float32).astype(jnp.bfloat16)
    grad_value_weight = jnp.dot(flattened.T, grad_values, preferred_element_type=jnp.float32).astype(jnp.bfloat16)
    group_cols = HK // N_SHARD

    def add_group(running, group_index):
        first_col = (group_index * group_cols).astype(jnp.int32)
        key_part = lax.dynamic_slice_in_dim(grad_keys, first_col, group_cols, 1)
        value_part = lax.dynamic_slice_in_dim(grad_values, first_col, group_cols, 1)
        key_cols = lax.dynamic_slice_in_dim(key_weight, first_col, group_cols, 1)
        value_cols = lax.dynamic_slice_in_dim(value_weight, first_col, group_cols, 1)
        partial_term = jnp.dot(key_part, key_cols.T, preferred_element_type=jnp.float32)
        partial_term = partial_term + jnp.dot(value_part, value_cols.T, preferred_element_type=jnp.float32)
        rounded = lax.optimization_barrier(partial_term.astype(jnp.bfloat16))
        return running + rounded.astype(jnp.float32), None

    start_sum = jnp.zeros((SLOTS * LS, D), jnp.float32)
    routed_grad, _ = lax.scan(add_group, start_sum, jnp.arange(N_SHARD, dtype=jnp.int32))
    routed_grad = routed_grad.astype(jnp.bfloat16).reshape(SLOTS, LS, D)
    return (context.reshape(SLOTS, LT, HK), grad_queries.reshape(SLOTS, LT, HK), routed_grad,
            grad_key_weight, grad_value_weight)


def reference(memory, lang_id, src_len, tgt_len, queries, key_weight, value_weight, grad_context):
    slot = route_slots(lang_id)
    routed = jnp.zeros((LANGS, SLOTS, LS, D), jnp.bfloat16).at[lang_id, slot].set(memory)
    src_slot = jnp.zeros((LANGS, SLOTS), jnp.int32).at[lang_id, slot].set(src_len)
    tgt_slot = jnp.zeros((LANGS, SLOTS), jnp.int32).at[lang_id, slot].set(tgt_len)
    context, grad_queries, routed_grad, grad_key_weight, grad_value_weight = lax.map(
        one_language, (routed, src_slot, tgt_slot, queries, key_weight, value_weight, grad_context))
    grad_memory = routed_grad[lang_id, slot]
    return context, grad_queries, grad_memory, grad_key_weight, grad_value_weight
```

```python
import jax
import jax.numpy as jnp
from jax import lax
from jax.experimental import pallas as pl
from jax.experimental.pallas import tpu as pltpu
from jax.sharding import Mesh, PartitionSpec as P

HEAD = 128
SRC = 16
TGT = 128
WIDTH = 4096
HALF = WIDTH // 2
PLANES = 8
SIDE = 4
CHIPS = SIDE * SIDE
ROWS = 32
GROUP = 8
MASKED = -1e30
BF = jnp.bfloat16
F32 = jnp.float32
PLANE = ("y", "x")
VMEM = pl.BlockSpec(memory_space=pltpu.VMEM)
SMEM = pl.BlockSpec(memory_space=pltpu.SMEM)
ANY = pl.BlockSpec(memory_space=pl.ANY)


def params(mib):
    return pltpu.CompilerParams(vmem_limit_bytes=mib << 20)


def shift(value, axis, step):
    n = lax.axis_size(axis)
    return lax.ppermute(value, axis, [(i, (i + step) % n) for i in range(n)])


def dot(a, b, ca, cb):
    return lax.dot_general(a, b, (((ca,), (cb,)), ((), ())), preferred_element_type=F32)


def route_kernel(place_ref, *refs):
    sentences, (routed_ref, rank_ref, lens_ref) = refs[:PLANES], refs[PLANES:]
    plane = place_ref[0]
    plane_f = plane.astype(F32)
    match, rank = [], []
    for ref in sentences:
        lang = ref[:, WIDTH : WIDTH + HEAD].astype(F32)
        match.append(jnp.where(lang == plane_f, 1.0, 0.0))
    origin = [lax.rem(plane - d + PLANES, PLANES) for d in range(PLANES)]
    for d in range(PLANES):
        before = jnp.zeros((SRC, HEAD), F32)
        for e in range(PLANES):
            if e != d:
                before += jnp.where(origin[e] < origin[d], match[e], 0.0)
        rank.append(jnp.where(match[d] > 0.5, before, -1.0))
        rank_ref[d] = rank[d][:8]
    for r in range(2):
        src = jnp.zeros((8, HEAD), F32)
        tgt = jnp.zeros((8, HEAD), F32)
        total = jnp.zeros((SRC, WIDTH), BF)
        for d, ref in enumerate(sentences):
            here = rank[d] == float(r)
            src = jnp.where(here[:8], ref[:8, WIDTH + HEAD : WIDTH + 2 * HEAD].astype(F32), src)
            tgt = jnp.where(here[:8], ref[:8, WIDTH + 2 * HEAD :].astype(F32), tgt)
            wide = jnp.where(here[:, :1], 1.0, 0.0).astype(BF)
            total = jnp.where(wide > 0.5, ref[:, :WIDTH], total)
        lens_ref[r] = src
        lens_ref[2 + r] = tgt
        routed_ref[r * SRC : (r + 1) * SRC] = total


def project_kernel(place_ref, *refs):
    blocks, weights, out_ref = refs[: 2 * SIDE], refs[2 * SIDE], refs[2 * SIDE + 1]
    rows, weight, part, sems = refs[2 * SIDE + 2 :]
    copies = []
    for half in range(2):
        copies.append(
            pltpu.make_async_copy(
                weights.at[pl.ds(half * HALF, HALF)], weight.at[half], sems.at[half]
            )
        )
    for i in range(2 * SIDE):
        span = pl.ds((i % SIDE) * SIDE * ROWS, SIDE * ROWS)
        copies.append(
            pltpu.make_async_copy(blocks[i], rows.at[i // SIDE, span], sems.at[2 + i])
        )
    for i in (0, *range(2, 2 + SIDE), 1, *range(2 + SIDE, 2 + 2 * SIDE)):
        copies[i].start()
    copies[0].wait()
    for i in range(2, 2 + SIDE):
        copies[i].wait()
    part[...] = dot(rows[0], weight[0], 1, 0)
    copies[1].wait()
    for i in range(2 + SIDE, 2 + 2 * SIDE):
        copies[i].wait()
    second = dot(rows[1], weight[1], 1, 0)
    y, x = place_ref[1], place_ref[2]
    for dy in range(SIDE):
        for dx in range(SIDE):
            a, b = (dy * SIDE + dx) * ROWS, (dx * SIDE + dy) * ROWS
            total = part[a : a + ROWS] + second[b : b + ROWS]
            chip = lax.rem(y - dy + SIDE, SIDE) * SIDE + lax.rem(x - dx + SIDE, SIDE)
            out_ref[chip] = total.astype(BF)


def attend_kernel(lens_ref, q_ref, g_ref, kv_ref, ctx_ref, gq_ref, gkv_ref, keys, values):
    slot, group = pl.program_id(0), pl.program_id(1)

    @pl.when((slot == 0) & (group == 0))
    def _():
        keys[...] = jnp.zeros_like(keys)
        values[...] = jnp.zeros_like(values)

    for h in range(GROUP):
        rows, cols = slice(h * SRC, (h + 1) * SRC), slice(h * HEAD, (h + 1) * HEAD)
        start = (h % 2) * 2 * HEAD
        keys[rows, cols] = kv_ref[h // 2, :, start : start + HEAD]
        values[rows, cols] = kv_ref[h // 2, :, start + HEAD : start + 2 * HEAD]
    scaling = HEAD ** (-0.5)
    split = (GROUP, SRC, TGT)
    src = jnp.maximum(lens_ref[slot][:1], 1.0)[None]
    tgt = lens_ref[2 + slot][:1, :1]
    q = q_ref[0]
    scores = (dot(keys[...], q, 1, 1) * scaling).reshape(split)
    key_index = lax.broadcasted_iota(jnp.int32, split, 1).astype(F32)
    scores = jnp.where(key_index < src, scores, MASKED)
    shifted = jnp.exp(scores - jnp.max(scores, axis=1, keepdims=True))
    attention = shifted / jnp.sum(shifted, axis=1, keepdims=True)
    attention_bf = attention.reshape(GROUP * SRC, TGT).astype(BF)
    row_index = lax.broadcasted_iota(jnp.int32, (TGT, 1), 0).astype(F32)
    valid = row_index < tgt
    context = dot(attention_bf, values[...], 0, 0)
    ctx_ref[0] = jnp.where(valid, context, 0.0).astype(BF)
    grad_masked = jnp.where(valid, g_ref[0].astype(F32), 0.0).astype(BF)
    grad_values = dot(attention_bf, grad_masked, 1, 0).astype(BF)
    grad_attention = dot(values[...], grad_masked, 1, 1).reshape(split)
    row_dot = jnp.sum(attention * grad_attention, axis=1, keepdims=True)
    grad_scores = (attention * (grad_attention - row_dot)).reshape(GROUP * SRC, TGT).astype(BF)
    gq_ref[0] = (dot(grad_scores, keys[...], 0, 0) * scaling).astype(BF)
    grad_keys = (dot(grad_scores, q, 1, 0) * scaling).astype(BF)
    for h in range(GROUP):
        rows, cols = slice(h * SRC, (h + 1) * SRC), slice(h * HEAD, (h + 1) * HEAD)
        start = (h % 2) * 2 * HEAD
        gkv_ref[h // 2, :, start : start + HEAD] = grad_keys[rows, cols]
        gkv_ref[h // 2, :, start + HEAD : start + 2 * HEAD] = grad_values[rows, cols]


def reorder_kernel(place_ref, grads_ref, by_y_ref, by_x_ref):
    y, x = place_ref[1], place_ref[2]
    for dy in range(SIDE):
        for dx in range(SIDE):
            chip = lax.rem(y - dy + SIDE, SIDE) * SIDE + lax.rem(x - dx + SIDE, SIDE)
            block = grads_ref[chip]
            by_y_ref[dy * SIDE + dx] = block
            by_x_ref[dx * SIDE + dy] = block


def give_back_kernel(rank_ref, a_ref, b_ref, *outs):
    for d, out in enumerate(outs):
        first = jnp.where(rank_ref[d][:1, :1] < 0.5, 1.0, 0.0).astype(BF)
        for i, ref in enumerate((a_ref, b_ref)):
            cols = slice(i * HALF, (i + 1) * HALF)
            out[:, cols] = jnp.where(first > 0.5, ref[:SRC], ref[SRC:])


def pick_kernel(place_ref, *refs):
    candidates, out_ref = refs[:PLANES], refs[PLANES]
    for d, ref in enumerate(candidates):

        @pl.when(place_ref[3] == d)
        def _():
            out_ref[...] = ref[...]


def local(memory, lang_id, src_len, tgt_len, queries, key_weight, value_weight, grad_context):
    plane, y, x = lax.axis_index("lang"), lax.axis_index("y"), lax.axis_index("x")
    core = lax.axis_index("core")
    ahead = lax.rem(lang_id[0] - plane + PLANES, PLANES)
    place = jnp.stack([plane, y, x, ahead]).astype(jnp.int32)

    def spread(number):
        return jnp.broadcast_to(number.astype(BF), (SRC, HEAD))

    with jax.named_scope("sentences_over_lang"):
        sentence = jnp.concatenate(
            [memory[0], spread(lang_id[0]), spread(src_len[0]), spread(tgt_len[0])], axis=1
        )
        column = [sentence] + [shift(sentence, "lang", d) for d in range(1, PLANES)]

    with jax.named_scope("weights_of_chip"):
        own_weight = jnp.concatenate([key_weight[0], value_weight[0]], axis=1)
        other_weight = shift(own_weight, "core", 1)
        weights = jnp.where(
            core == 0,
            jnp.concatenate([own_weight, other_weight], axis=1),
            jnp.concatenate([other_weight, own_weight], axis=1),
        )

    with jax.named_scope("route"):
        routed, rank, lens = pl.pallas_call(
            route_kernel,
            out_shape=(
                jax.ShapeDtypeStruct((ROWS, WIDTH), BF),
                jax.ShapeDtypeStruct((PLANES, 8, HEAD), F32),
                jax.ShapeDtypeStruct((4, 8, HEAD), F32),
            ),
            in_specs=[SMEM] + [VMEM] * PLANES,
            out_specs=(VMEM, VMEM, VMEM),
            compiler_params=params(16),
        )(place, *column)

    with jax.named_scope("gather_rows"):
        halves = []
        for half, (first, second) in enumerate((("x", "y"), ("y", "x"))):
            own = routed[:, half * HALF : (half + 1) * HALF]
            line = [own] + [shift(own, first, d) for d in range(1, SIDE)]
            halves.append((jnp.concatenate(line, axis=0), second))
        blocks = []
        for line, second in halves:
            blocks += [line] + [shift(line, second, d) for d in range(1, SIDE)]

    with jax.named_scope("project"):
        projected = pl.pallas_call(
            project_kernel,
            out_shape=jax.ShapeDtypeStruct((CHIPS, ROWS, 4 * HEAD), BF),
            in_specs=[SMEM] + [ANY] * (2 * SIDE + 1),
            out_specs=VMEM,
            scratch_shapes=[
                pltpu.VMEM((2, CHIPS * ROWS, HALF), BF),
                pltpu.VMEM((2, HALF, 4 * HEAD), BF),
                pltpu.VMEM((CHIPS * ROWS, 4 * HEAD), F32),
                pltpu.SemaphoreType.DMA((2 + 2 * SIDE,)),
            ],
            compiler_params=params(32),
        )(place, *blocks, weights)

    with jax.named_scope("rows_to_slots"):
        slot_rows = lax.all_to_all(projected, PLANE, 0, 0, tiled=True)

    with jax.named_scope("attend"):
        groups = WIDTH // (GROUP * HEAD)
        wide = pl.BlockSpec((1, TGT, GROUP * HEAD), lambda s, g: (s, 0, g))
        narrow = pl.BlockSpec((GROUP // 2, SRC, 4 * HEAD), lambda s, g: (g, s, 0))
        context, grad_queries, slot_grads = pl.pallas_call(
            attend_kernel,
            grid=(2, groups),
            out_shape=(
                jax.ShapeDtypeStruct((2, TGT, WIDTH), BF),
                jax.ShapeDtypeStruct((2, TGT, WIDTH), BF),
                jax.ShapeDtypeStruct((CHIPS, ROWS, 4 * HEAD), BF),
            ),
            in_specs=[VMEM, wide, wide, narrow],
            out_specs=(wide, wide, narrow),
            scratch_shapes=[
                pltpu.VMEM((GROUP * SRC, GROUP * HEAD), BF),
                pltpu.VMEM((GROUP * SRC, GROUP * HEAD), BF),
            ],
            compiler_params=params(32),
        )(lens, queries[0], grad_context[0], slot_rows)

    with jax.named_scope("grads_to_heads"):
        head_grads = lax.all_to_all(slot_grads, PLANE, 0, 0, tiled=True)
        by_y, by_x = pl.pallas_call(
            reorder_kernel,
            out_shape=(jax.ShapeDtypeStruct((CHIPS, ROWS, 4 * HEAD), BF),) * 2,
            in_specs=[SMEM, VMEM],
            out_specs=(VMEM, VMEM),
            compiler_params=params(16),
        )(place, head_grads)
        by_y = by_y.reshape(CHIPS * ROWS, 4 * HEAD)
        by_x = by_x.reshape(CHIPS * ROWS, 4 * HEAD)

    with jax.named_scope("sum_rows"):
        width = SIDE * ROWS
        partial = []
        for half, (grads, first) in enumerate(((by_x, "x"), (by_y, "y"))):
            weight = weights[half * HALF : (half + 1) * HALF]
            terms = [
                dot(grads[d * width : (d + 1) * width], weight, 1, 1).astype(BF)
                for d in range(SIDE)
            ]
            partial.append([terms[0]] + [shift(terms[d], first, -d) for d in range(1, SIDE)])
        summed = []
        for half, second in enumerate(("y", "x")):
            line = sum(term.astype(F32) for term in partial[half]).astype(BF)
            terms = [line[d * ROWS : (d + 1) * ROWS] for d in range(SIDE)]
            terms = [terms[0]] + [shift(terms[d], second, -d) for d in range(1, SIDE)]
            summed.append(sum(term.astype(F32) for term in terms).astype(BF))

    with jax.named_scope("weight_grads"):
        parts = []
        for half, grads in enumerate((by_y, by_x)):
            rows = jnp.concatenate(blocks[half * SIDE : (half + 1) * SIDE], axis=0)
            parts.append(dot(rows, grads, 0, 0).astype(BF))
        both = jnp.concatenate(parts, axis=0)
        low, high = both[:, : 2 * HEAD], both[:, 2 * HEAD :]
        keep = jnp.where(core == 0, low, high)
        arrived = shift(jnp.where(core == 0, high, low), "core", 1)
        total = (keep.astype(F32) + arrived.astype(F32)).astype(BF)
        grad_key_weight, grad_value_weight = total[:, :HEAD], total[:, HEAD:]

    with jax.named_scope("sentences_back"):
        sends = pl.pallas_call(
            give_back_kernel,
            out_shape=(jax.ShapeDtypeStruct((SRC, WIDTH), BF),) * PLANES,
            in_specs=[VMEM] * 3,
            out_specs=(VMEM,) * PLANES,
            compiler_params=params(16),
        )(rank, *summed)
        candidates = [sends[0]] + [shift(sends[d], "lang", -d) for d in range(1, PLANES)]
        grad_memory = pl.pallas_call(
            pick_kernel,
            out_shape=jax.ShapeDtypeStruct((SRC, WIDTH), BF),
            in_specs=[SMEM] + [VMEM] * PLANES,
            out_specs=VMEM,
            compiler_params=params(16),
        )(place, *candidates)

    return (
        context[None],
        grad_queries[None],
        grad_memory[None],
        grad_key_weight[None],
        grad_value_weight[None],
    )


def solution(mesh):
    planes = mesh.shape["lang"]
    grid = Mesh(mesh.devices.reshape(planes, SIDE, SIDE, 2), ("lang", "y", "x", "core"))
    shard = ("y", "x", "core")
    every = ("lang", "y", "x", "core")
    return jax.shard_map(
        local,
        mesh=grid,
        in_specs=(
            P(every, None, None),
            P(every),
            P(every),
            P(every),
            P("lang", shard, None, None),
            P("lang", None, shard),
            P("lang", None, shard),
            P("lang", shard, None, None),
        ),
        out_specs=(
            P("lang", shard, None, None),
            P("lang", shard, None, None),
            P(every, None, None),
            P("lang", None, shard),
            P("lang", None, shard),
        ),
        check_vma=False,
    )
```

```python
import functools

import jax
import jax.numpy as jnp
from jax import lax
from jax.experimental import pallas as pl
from jax.experimental.pallas import tpu as pltpu
from jax.sharding import Mesh, PartitionSpec as P

HEAD = 128
SRC = 16
TGT = 128
WIDTH = 4096
HALF = WIDTH // 2
PLANES = 8
SIDE = 4
CHIPS = SIDE * SIDE
ROWS = 32
GROUP = 8
MASKED = -1e30
BF = jnp.bfloat16
F32 = jnp.float32
PLANE = ("y", "x")
FAR_FIRST = (0, 4, 3, 5, 2, 6, 1, 7)
TAKEN = ((0, 0), (1, 0), (0, 2), (1, 2), (0, 1), (1, 1), (0, 3), (1, 3))
VMEM = pl.BlockSpec(memory_space=pltpu.VMEM)
SMEM = pl.BlockSpec(memory_space=pltpu.SMEM)
ANY = pl.BlockSpec(memory_space=pl.ANY)


def params(mib):
    return pltpu.CompilerParams(vmem_limit_bytes=mib << 20)


def cost(products, mib):
    return pl.CostEstimate(flops=2 * products, bytes_accessed=mib << 20, transcendentals=0)


def shift(value, axis, step):
    n = lax.axis_size(axis)
    return lax.ppermute(value, axis, [(i, (i + step) % n) for i in range(n)])


def dot(a, b, ca, cb):
    return lax.dot_general(a, b, (((ca,), (cb,)), ((), ())), preferred_element_type=F32)


def route_kernel(place_ref, *refs):
    sentences, (left_ref, right_ref, rank_ref, lens_ref) = refs[:PLANES], refs[PLANES:]
    sentences = [sentences[FAR_FIRST.index(d)] for d in range(PLANES)]
    plane = place_ref[0]
    plane_f = plane.astype(F32)
    match, rank = [], []
    for ref in sentences:
        lang = ref[:, WIDTH : WIDTH + HEAD].astype(F32)
        match.append(jnp.where(lang == plane_f, 1.0, 0.0))
    origin = [lax.rem(plane - d + PLANES, PLANES) for d in range(PLANES)]
    for d in range(PLANES):
        before = jnp.zeros((SRC, HEAD), F32)
        for e in range(PLANES):
            if e != d:
                before += jnp.where(origin[e] < origin[d], match[e], 0.0)
        rank.append(jnp.where(match[d] > 0.5, before, -1.0))
        rank_ref[d] = rank[d][:8]
    for r in range(2):
        src = jnp.zeros((8, HEAD), F32)
        tgt = jnp.zeros((8, HEAD), F32)
        total = jnp.zeros((SRC, WIDTH), BF)
        for d, ref in enumerate(sentences):
            here = rank[d] == float(r)
            src = jnp.where(here[:8], ref[:8, WIDTH + HEAD : WIDTH + 2 * HEAD].astype(F32), src)
            tgt = jnp.where(here[:8], ref[:8, WIDTH + 2 * HEAD :].astype(F32), tgt)
            wide = jnp.where(here[:, :1], 1.0, 0.0).astype(BF)
            total = jnp.where(wide > 0.5, ref[:, :WIDTH], total)
        lens_ref[r] = src
        lens_ref[2 + r] = tgt
        left_ref[r * SRC : (r + 1) * SRC] = total[:, :HALF]
        right_ref[r * SRC : (r + 1) * SRC] = total[:, HALF:]


def join_kernel(*refs):
    parts, outs, sems = refs[: 2 * SIDE], refs[2 * SIDE : 2 * SIDE + 2], refs[2 * SIDE + 2]
    copies = [
        pltpu.make_async_copy(part, outs[half].at[pl.ds(d * ROWS, ROWS)], sems.at[i])
        for i, (part, (half, d)) in enumerate(zip(parts, TAKEN))
    ]
    for copy in copies:
        copy.start()
    for copy in copies:
        copy.wait()


def shift_both(values, axes, sign, order):
    moved = [[terms[0], None, None, None] for terms in values]
    for half, d in order:
        if d:
            moved[half][d] = shift(values[half][d], axes[half], sign * d)
    return moved


def project_kernel(place_ref, *refs):
    blocks, (own_ref, other_ref, out_ref) = refs[: 2 * SIDE], refs[2 * SIDE : 2 * SIDE + 3]
    blocks = [blocks[TAKEN.index(divmod(i, SIDE))] for i in range(2 * SIDE)]
    rows, weight, part, weight_sems, row_sems = refs[2 * SIDE + 3 :]
    weight_copies, row_copies = [], []
    for half in range(2):
        for i, ref in enumerate((own_ref, other_ref)):
            weight_copies.append(
                pltpu.make_async_copy(
                    ref.at[pl.ds(half * HALF, HALF)],
                    weight.at[half, i],
                    weight_sems.at[2 * half + i],
                )
            )
    for i in range(2 * SIDE):
        span = pl.ds((i % SIDE) * SIDE * ROWS, SIDE * ROWS)
        row_copies.append(
            pltpu.make_async_copy(blocks[i], rows.at[i // SIDE, span], row_sems.at[i])
        )
    for half in range(2):
        for copy in weight_copies[2 * half : 2 * half + 2] + row_copies[SIDE * half : SIDE * half + SIDE]:
            copy.start()
    for half in range(2):
        for copy in weight_copies[2 * half : 2 * half + 2] + row_copies[SIDE * half : SIDE * half + SIDE]:
            copy.wait()
        for i in range(2):
            part[half, :, i * 2 * HEAD : (i + 1) * 2 * HEAD] = dot(rows[half], weight[half, i], 1, 0)
    y, x = place_ref[1], place_ref[2]
    for dy in range(SIDE):
        for dx in range(SIDE):
            a, b = (dy * SIDE + dx) * ROWS, (dx * SIDE + dy) * ROWS
            total = part[0, a : a + ROWS] + part[1, b : b + ROWS]
            chip = lax.rem(y - dy + SIDE, SIDE) * SIDE + lax.rem(x - dx + SIDE, SIDE)
            out_ref[chip] = total.astype(BF)


def attend_kernel(place_ref, lens_ref, q_ref, g_ref, kv_ref, ctx_ref, gq_ref, gkv_ref, keys, values):
    swapped = place_ref[4] == 1
    scaling = HEAD ** (-0.5)
    split = (GROUP, SRC, TGT)

    @pl.when(pl.program_id(0) == 0)
    def _():
        keys[...] = jnp.zeros_like(keys)
        values[...] = jnp.zeros_like(values)

    for s in range(2):
        slot = slice(s * SRC, (s + 1) * SRC)
        for h in range(GROUP):
            rows, cols = slice(h * SRC, (h + 1) * SRC), slice(h * HEAD, (h + 1) * HEAD)
            own, other = (h % 2) * 2 * HEAD, (1 - h % 2) * 2 * HEAD
            for start, block in ((0, keys), (HEAD, values)):
                block[s, rows, cols] = jnp.where(
                    swapped,
                    kv_ref[h // 2, slot, other + start : other + start + HEAD],
                    kv_ref[h // 2, slot, own + start : own + start + HEAD],
                )
    grads = []
    for s in range(2):
        src = jnp.maximum(lens_ref[s][:1], 1.0)[None]
        tgt = lens_ref[2 + s][:1, :1]
        q = q_ref[s]
        scores = (dot(keys[s], q, 1, 1) * scaling).reshape(split)
        key_index = lax.broadcasted_iota(jnp.int32, split, 1).astype(F32)
        scores = jnp.where(key_index < src, scores, MASKED)
        shifted = jnp.exp(scores - jnp.max(scores, axis=1, keepdims=True))
        attention = shifted / jnp.sum(shifted, axis=1, keepdims=True)
        attention_bf = attention.reshape(GROUP * SRC, TGT).astype(BF)
        row_index = lax.broadcasted_iota(jnp.int32, (TGT, 1), 0).astype(F32)
        valid = row_index < tgt
        valid_bf = jnp.where(valid, 1.0, 0.0).astype(BF)
        context = dot(attention_bf, values[s], 0, 0)
        ctx_ref[s] = jnp.where(valid, context, 0.0).astype(BF)
        g = g_ref[s]
        grad_masked = jnp.where(valid_bf > 0.5, g, jnp.zeros_like(g))
        grad_values = dot(attention_bf, grad_masked, 1, 0)
        grad_attention = dot(values[s], grad_masked, 1, 1).reshape(split)
        row_dot = jnp.sum(attention * grad_attention, axis=1, keepdims=True)
        grad_scores = (attention * (grad_attention - row_dot)).reshape(GROUP * SRC, TGT).astype(BF)
        gq_ref[s] = (dot(grad_scores, keys[s], 0, 0) * scaling).astype(BF)
        grad_keys = dot(grad_scores, q, 1, 0) * scaling
        grads.append((grad_keys, grad_values))
    for s in range(2):
        slot = slice(s * SRC, (s + 1) * SRC)
        for p in range(GROUP // 2):
            for start, grad in ((0, grads[s][0]), (HEAD, grads[s][1])):
                low, high = (
                    grad[h * SRC : (h + 1) * SRC, h * HEAD : (h + 1) * HEAD].astype(BF)
                    for h in (2 * p, 2 * p + 1)
                )
                gkv_ref[p, slot, start : start + HEAD] = jnp.where(swapped, high, low)
                start += 2 * HEAD
                gkv_ref[p, slot, start : start + HEAD] = jnp.where(swapped, low, high)


def chip_at(place_ref, dy, dx):
    y, x = place_ref[1], place_ref[2]
    return lax.rem(y - dy + SIDE, SIDE) * SIDE + lax.rem(x - dx + SIDE, SIDE)


def reorder_kernel(place_ref, grads_ref, by_y_ref, by_x_ref):
    for dy in range(SIDE):
        for dx in range(SIDE):
            block = grads_ref[chip_at(place_ref, dy, dx)]
            by_y_ref[dy * SIDE + dx] = block
            by_x_ref[dx * SIDE + dy] = block


def partial_kernel(along_y, place_ref, grads_ref, own_ref, other_ref, *refs):
    outs, grads = refs[:SIDE], refs[SIDE]

    @pl.when(pl.program_id(0) == 0)
    def _():
        for d in range(SIDE):
            for e in range(SIDE):
                chip = chip_at(place_ref, *((d, e) if along_y else (e, d)))
                start = (d * SIDE + e) * ROWS
                grads[start : start + ROWS] = grads_ref[chip]

    total = dot(grads[:, : 2 * HEAD], own_ref[...], 1, 1)
    total += dot(grads[:, 2 * HEAD :], other_ref[...], 1, 1)
    for d, out in enumerate(outs):
        out[...] = total[d * SIDE * ROWS : (d + 1) * SIDE * ROWS].astype(BF)


def weight_kernel(by_y_ref, by_x_ref, *refs):
    blocks, (own_ref, other_ref) = refs[: 2 * SIDE], refs[2 * SIDE :]
    step = pl.program_id(0)
    for half, grads in enumerate((by_y_ref, by_x_ref)):

        @pl.when((step >= half * SIDE) & (step < (half + 1) * SIDE))
        def _():
            rows = jnp.concatenate([ref[...] for ref in blocks[half * SIDE : (half + 1) * SIDE]], axis=0)
            total = dot(rows, grads[...], 0, 0).astype(BF)
            own_ref[...] = total[:, : 2 * HEAD]
            other_ref[...] = total[:, 2 * HEAD :]


def give_back_kernel(rank_ref, a_ref, b_ref, *outs):
    for d, out in enumerate(outs):
        first = jnp.where(rank_ref[d][:1, :1] < 0.5, 1.0, 0.0).astype(BF)
        for i, ref in enumerate((a_ref, b_ref)):
            cols = slice(i * HALF, (i + 1) * HALF)
            out[:, cols] = jnp.where(first > 0.5, ref[:SRC], ref[SRC:])


def pick_kernel(place_ref, *refs):
    candidates, out_ref = refs[:PLANES], refs[PLANES]
    for d, ref in zip(FAR_FIRST, candidates):

        @pl.when(place_ref[3] == d)
        def _():
            out_ref[...] = ref[...]


def local(memory, lang_id, src_len, tgt_len, queries, key_weight, value_weight, grad_context):
    plane, y, x = lax.axis_index("lang"), lax.axis_index("y"), lax.axis_index("x")
    core = lax.axis_index("core")
    ahead = lax.rem(lang_id[0] - plane + PLANES, PLANES)
    place = jnp.stack([plane, y, x, ahead, core]).astype(jnp.int32)

    def spread(number):
        return jnp.broadcast_to(number.astype(BF), (SRC, HEAD))

    with jax.named_scope("sentences_over_lang"):
        sentence = jnp.concatenate(
            [memory[0], spread(lang_id[0]), spread(src_len[0]), spread(tgt_len[0])], axis=1
        )
        column = [sentence] + [shift(sentence, "lang", d) for d in FAR_FIRST[1:]]

    with jax.named_scope("weights_of_chip"):
        key_own, value_own, _ = lax.optimization_barrier((key_weight[0], value_weight[0], sentence))
        own_weight = jnp.concatenate([key_own, value_own], axis=1)
        other_weight = shift(own_weight, "core", 1)

    with jax.named_scope("route"):
        left, right, rank, lens = pl.pallas_call(
            route_kernel,
            out_shape=(
                jax.ShapeDtypeStruct((ROWS, HALF), BF),
                jax.ShapeDtypeStruct((ROWS, HALF), BF),
                jax.ShapeDtypeStruct((PLANES, 8, HEAD), F32),
                jax.ShapeDtypeStruct((4, 8, HEAD), F32),
            ),
            in_specs=[SMEM] + [VMEM] * PLANES,
            out_specs=(VMEM,) * 4,
            compiler_params=params(16),
        )(place, *column)

    with jax.named_scope("gather_rows"):
        left, right, own_weight, other_weight = lax.optimization_barrier(
            (left, right, own_weight, other_weight)
        )
        parts = shift_both([[left] * SIDE, [right] * SIDE], ("x", "y"), 1, TAKEN)
        lines = pl.pallas_call(
            join_kernel,
            out_shape=(jax.ShapeDtypeStruct((SIDE * ROWS, HALF), BF),) * 2,
            in_specs=[ANY] * (2 * SIDE),
            out_specs=(ANY, ANY),
            scratch_shapes=[pltpu.SemaphoreType.DMA((2 * SIDE,))],
            compiler_params=params(1),
        )(*[parts[half][d] for half, d in TAKEN])
        blocks = shift_both([[line] * SIDE for line in lines], ("y", "x"), 1, TAKEN)
        blocks = [*blocks[0], *blocks[1]]

    with jax.named_scope("project"):
        projected = pl.pallas_call(
            project_kernel,
            out_shape=jax.ShapeDtypeStruct((CHIPS, ROWS, 4 * HEAD), BF),
            in_specs=[SMEM] + [ANY] * (2 * SIDE + 2),
            out_specs=VMEM,
            scratch_shapes=[
                pltpu.VMEM((2, CHIPS * ROWS, HALF), BF),
                pltpu.VMEM((2, 2, HALF, 2 * HEAD), BF),
                pltpu.VMEM((2, CHIPS * ROWS, 4 * HEAD), F32),
                pltpu.SemaphoreType.DMA((4,)),
                pltpu.SemaphoreType.DMA((2 * SIDE,)),
            ],
            compiler_params=params(40),
        )(place, *[blocks[half * SIDE + d] for half, d in TAKEN], own_weight, other_weight)

    with jax.named_scope("rows_to_slots"):
        slot_rows = lax.all_to_all(projected, PLANE, 0, 0, tiled=True)

    with jax.named_scope("attend"):
        groups = WIDTH // (GROUP * HEAD)
        wide = pl.BlockSpec((2, TGT, GROUP * HEAD), lambda g: (0, 0, g))
        narrow = pl.BlockSpec((GROUP // 2, ROWS, 4 * HEAD), lambda g: (g, 0, 0))
        context, grad_queries, slot_grads = pl.pallas_call(
            attend_kernel,
            grid=(groups,),
            out_shape=(
                jax.ShapeDtypeStruct((2, TGT, WIDTH), BF),
                jax.ShapeDtypeStruct((2, TGT, WIDTH), BF),
                jax.ShapeDtypeStruct((CHIPS, ROWS, 4 * HEAD), BF),
            ),
            in_specs=[SMEM, VMEM, wide, wide, narrow],
            out_specs=(wide, wide, narrow),
            scratch_shapes=[
                pltpu.VMEM((2, GROUP * SRC, GROUP * HEAD), BF),
                pltpu.VMEM((2, GROUP * SRC, GROUP * HEAD), BF),
            ],
            compiler_params=params(58),
        )(place, lens, queries[0], grad_context[0], slot_rows)

    with jax.named_scope("grads_to_heads"):
        head_grads = lax.all_to_all(slot_grads, PLANE, 0, 0, tiled=True)

    with jax.named_scope("sum_rows"):
        tile = HALF // SIDE
        partial = []
        for half, first in enumerate(("x", "y")):
            weight_spec = pl.BlockSpec((tile, 2 * HEAD), lambda t, half=half: (half * SIDE + t, 0))
            terms = pl.pallas_call(
                functools.partial(partial_kernel, first == "y"),
                grid=(SIDE,),
                out_shape=(jax.ShapeDtypeStruct((SIDE * ROWS, HALF), BF),) * SIDE,
                in_specs=[SMEM, VMEM, weight_spec, weight_spec],
                out_specs=(pl.BlockSpec((SIDE * ROWS, tile), lambda t: (0, t)),) * SIDE,
                scratch_shapes=[pltpu.VMEM((CHIPS * ROWS, 4 * HEAD), BF)],
                compiler_params=params(24),
            )(place, head_grads, own_weight, other_weight)
            partial.append(terms)
        arrived = shift_both(partial, ("x", "y"), -1, TAKEN)

    with jax.named_scope("weight_grads"):
        head_grads, _ = lax.optimization_barrier((head_grads, partial))
        by_y, by_x = pl.pallas_call(
            reorder_kernel,
            out_shape=(jax.ShapeDtypeStruct((CHIPS, ROWS, 4 * HEAD), BF),) * 2,
            in_specs=[SMEM, VMEM],
            out_specs=(VMEM, VMEM),
            compiler_params=params(16),
        )(place, head_grads)
        block_specs = [
            pl.BlockSpec(
                (SIDE * ROWS, tile),
                lambda t, low=half * SIDE: (0, jnp.clip(t - low, 0, SIDE - 1)),
            )
            for half in range(2)
            for _ in range(SIDE)
        ]
        keep, send = pl.pallas_call(
            weight_kernel,
            grid=(2 * SIDE,),
            out_shape=(jax.ShapeDtypeStruct((WIDTH, 2 * HEAD), BF),) * 2,
            in_specs=[VMEM, VMEM] + block_specs,
            out_specs=(pl.BlockSpec((tile, 2 * HEAD), lambda t: (t, 0)),) * 2,
            compiler_params=params(32),
            cost_estimate=cost(CHIPS * ROWS * WIDTH * 4 * HEAD, 16),
        )(by_y.reshape(CHIPS * ROWS, 4 * HEAD), by_x.reshape(CHIPS * ROWS, 4 * HEAD), *blocks)
        both = shift(send, "core", 1)
        weight_grads = [
            (keep[:, cols].astype(F32) + both[:, cols].astype(F32)).astype(BF)
            for cols in (slice(0, HEAD), slice(HEAD, 2 * HEAD))
        ]

    with jax.named_scope("sum_rows"):
        lines = [sum(term.astype(F32) for term in terms).astype(BF) for terms in arrived]
        terms = [[line[d * ROWS : (d + 1) * ROWS] for d in range(SIDE)] for line in lines]
        arrived = shift_both(terms, ("y", "x"), -1, TAKEN)
        summed = [sum(term.astype(F32) for term in terms).astype(BF) for terms in arrived]
        summed, weight_grads = lax.optimization_barrier((summed, weight_grads))

    with jax.named_scope("sentences_back"):
        sends = pl.pallas_call(
            give_back_kernel,
            out_shape=(jax.ShapeDtypeStruct((SRC, WIDTH), BF),) * PLANES,
            in_specs=[VMEM] * 3,
            out_specs=(VMEM,) * PLANES,
            compiler_params=params(16),
        )(rank, *summed)
        candidates = [sends[0]] + [shift(sends[d], "lang", -d) for d in FAR_FIRST[1:]]
        grad_memory = pl.pallas_call(
            pick_kernel,
            out_shape=jax.ShapeDtypeStruct((SRC, WIDTH), BF),
            in_specs=[SMEM] + [VMEM] * PLANES,
            out_specs=VMEM,
            compiler_params=params(16),
        )(place, *candidates)

    return (
        context[None],
        grad_queries[None],
        grad_memory[None],
        weight_grads[0][None],
        weight_grads[1][None],
    )


def solution(mesh):
    planes = mesh.shape["lang"]
    grid = Mesh(mesh.devices.reshape(planes, SIDE, SIDE, 2), ("lang", "y", "x", "core"))
    shard = ("y", "x", "core")
    every = ("lang", "y", "x", "core")
    return jax.shard_map(
        local,
        mesh=grid,
        in_specs=(
            P(every, None, None),
            P(every),
            P(every),
            P(every),
            P("lang", shard, None, None),
            P("lang", None, shard),
            P("lang", None, shard),
            P("lang", shard, None, None),
        ),
        out_specs=(
            P("lang", shard, None, None),
            P("lang", shard, None, None),
            P(every, None, None),
            P("lang", None, shard),
            P("lang", None, shard),
        ),
        check_vma=False,
    )
```

```python
import functools

import jax
import jax.numpy as jnp
from jax import lax
from jax.experimental import pallas as pl
from jax.experimental.pallas import tpu as pltpu
from jax.sharding import Mesh, PartitionSpec as P

HEAD = 128
SRC = 16
TGT = 128
WIDTH = 4096
PLANES = 8
SIDE = 4
CHIPS = SIDE * SIDE
ROWS = 32
GROUP = 8
MASKED = -1e30
BF = jnp.bfloat16
F32 = jnp.float32
PLANE = ("y", "x")
FAR_FIRST = (0, 4, 3, 5, 2, 6, 1, 7)
LINE = (0, 2, 1, 3)
VMEM = pl.BlockSpec(memory_space=pltpu.VMEM)
SMEM = pl.BlockSpec(memory_space=pltpu.SMEM)
ANY = pl.BlockSpec(memory_space=pl.ANY)


def params(mib):
    return pltpu.CompilerParams(vmem_limit_bytes=mib << 20)


def cost(products, mib):
    return pl.CostEstimate(flops=2 * products, bytes_accessed=mib << 20, transcendentals=0)


def exchange(value):
    return lax.ppermute(value, "core", [(0, 1), (1, 0)])


def shift_lang(value, step):
    pairs = [
        (2 * z + c, 2 * ((z + (step if c == 0 else -step)) % PLANES) + c)
        for z in range(PLANES)
        for c in range(2)
    ]
    return lax.ppermute(value, ("lang", "core"), pairs)


def shift_plane(value, phase, step):
    pairs = []
    for y in range(SIDE):
        for x in range(SIDE):
            for c in range(2):
                along_x = c == phase
                to_y = y if along_x else (y + step) % SIDE
                to_x = (x + step) % SIDE if along_x else x
                pairs.append(((y * SIDE + x) * 2 + c, (to_y * SIDE + to_x) * 2 + c))
    return lax.ppermute(value, ("y", "x", "core"), pairs)


def dot(a, b, ca, cb):
    return lax.dot_general(a, b, (((ca,), (cb,)), ((), ())), preferred_element_type=F32)


def chip_at(place_ref, first, second):
    y, x, core = place_ref[1], place_ref[2], place_ref[4]
    dy = jnp.where(core == 0, second, first)
    dx = jnp.where(core == 0, first, second)
    return lax.rem(y - dy + SIDE, SIDE) * SIDE + lax.rem(x - dx + SIDE, SIDE)


def route_kernel(place_ref, *refs):
    sentences, (routed_ref, rank_ref, lens_ref) = refs[:PLANES], refs[PLANES:]
    sentences = [sentences[FAR_FIRST.index(d)] for d in range(PLANES)]
    plane, core = place_ref[0], place_ref[4]
    plane_f = plane.astype(F32)
    match, rank = [], []
    for ref in sentences:
        lang = ref[:, WIDTH : WIDTH + 1].astype(F32)
        match.append(jnp.where(lang == plane_f, 1.0, 0.0))
    origin = [
        lax.rem(plane + jnp.where(core == 0, PLANES - d, d), PLANES) for d in range(PLANES)
    ]
    for d in range(PLANES):
        before = jnp.zeros((SRC, 1), F32)
        for e in range(PLANES):
            if e != d:
                before += jnp.where(origin[e] < origin[d], match[e], 0.0)
        rank.append(jnp.where(match[d] > 0.5, before, -1.0))
        rank_ref[d] = jnp.broadcast_to(rank[d][:8], (8, HEAD))
    for r in range(2):
        src = jnp.zeros((8, 1), F32)
        tgt = jnp.zeros((8, 1), F32)
        total = jnp.zeros((SRC, WIDTH), BF)
        for d, ref in enumerate(sentences):
            here = rank[d] == float(r)
            src = jnp.where(here[:8], ref[:8, WIDTH + 1 : WIDTH + 2].astype(F32), src)
            tgt = jnp.where(here[:8], ref[:8, WIDTH + 2 : WIDTH + 3].astype(F32), tgt)
            wide = jnp.where(here, 1.0, 0.0).astype(BF)
            total = jnp.where(wide > 0.5, ref[:, :WIDTH], total)
        lens_ref[r] = jnp.broadcast_to(src, (8, HEAD))
        lens_ref[2 + r] = jnp.broadcast_to(tgt, (8, HEAD))
        routed_ref[r * SRC : (r + 1) * SRC] = total


def join_kernel(*refs):
    parts, out, sems = refs[:SIDE], refs[SIDE], refs[SIDE + 1]
    copies = [
        pltpu.make_async_copy(part, out.at[pl.ds(d * ROWS, ROWS)], sems.at[i])
        for i, (part, d) in enumerate(zip(parts, LINE))
    ]
    for copy in copies:
        copy.start()
    for copy in copies:
        copy.wait()


def project_kernel(place_ref, *refs):
    blocks, (own_ref, other_ref, out_ref) = refs[:SIDE], refs[SIDE : SIDE + 3]
    rows, weight, part, sems = refs[SIDE + 3 :]
    step = WIDTH // SIDE
    copies = []
    for k in range(SIDE):
        span = pl.ds(k * step, step)
        chunk = []
        for i, ref in enumerate((own_ref, other_ref)):
            chunk.append(pltpu.make_async_copy(ref.at[span], weight.at[k, i], sems.at[k, i]))
        for i, (ref, d) in enumerate(zip(blocks, LINE)):
            into = rows.at[k, pl.ds(d * SIDE * ROWS, SIDE * ROWS)]
            chunk.append(pltpu.make_async_copy(ref.at[:, span], into, sems.at[k, 2 + i]))
        copies.append(chunk)
        for copy in chunk:
            copy.start()
    for k, chunk in enumerate(copies):
        for copy in chunk:
            copy.wait()
        for i in range(2):
            cols = slice(i * 2 * HEAD, (i + 1) * 2 * HEAD)
            term = dot(rows[k], weight[k, i], 1, 0)
            part[:, cols] = term if k == 0 else part[:, cols] + term
    for second in range(SIDE):
        for first in range(SIDE):
            start = (second * SIDE + first) * ROWS
            chip = chip_at(place_ref, first, second)
            out_ref[chip] = part[start : start + ROWS].astype(BF)


def attend_kernel(place_ref, lens_ref, q_ref, g_ref, kv_ref, ctx_ref, gq_ref, gkv_ref, keys, values):
    swapped = place_ref[4] == 1
    scaling = HEAD ** (-0.5)
    split = (GROUP, SRC, TGT)

    @pl.when(pl.program_id(0) == 0)
    def _():
        keys[...] = jnp.zeros_like(keys)
        values[...] = jnp.zeros_like(values)

    def head(array, h):
        return array[:, h * HEAD : (h + 1) * HEAD]

    for s in range(2):
        slot = slice(s * SRC, (s + 1) * SRC)
        for h in range(GROUP):
            rows, cols = slice(h * SRC, (h + 1) * SRC), slice(h * HEAD, (h + 1) * HEAD)
            own, other = (h % 2) * 2 * HEAD, (1 - h % 2) * 2 * HEAD
            for start, block in ((0, keys), (HEAD, values)):
                block[s, rows, cols] = jnp.where(
                    swapped,
                    kv_ref[h // 2, slot, other + start : other + start + HEAD],
                    kv_ref[h // 2, slot, own + start : own + start + HEAD],
                )
    grads = []
    for s in range(2):
        src = jnp.maximum(lens_ref[s][:1], 1.0)[None]
        tgt = lens_ref[2 + s][:1, :1]
        q, g = q_ref[s], g_ref[s]
        row_index = lax.broadcasted_iota(jnp.int32, (TGT, 1), 0).astype(F32)
        valid = row_index < tgt
        valid_bf = jnp.where(valid, 1.0, 0.0).astype(BF)
        grad_masked = jnp.where(valid_bf > 0.5, g, jnp.zeros_like(g))
        scores = (dot(keys[s], q, 1, 1) * scaling).reshape(split)
        key_index = lax.broadcasted_iota(jnp.int32, split, 1).astype(F32)
        scores = jnp.where(key_index < src, scores, MASKED)
        shifted = jnp.exp(scores - jnp.max(scores, axis=1, keepdims=True))
        attention = shifted / jnp.sum(shifted, axis=1, keepdims=True)
        attention_bf = attention.astype(BF)
        context = dot(attention_bf.reshape(GROUP * SRC, TGT), values[s], 0, 0)
        ctx_ref[s] = jnp.where(valid, context, 0.0).astype(BF)
        grad_attention = dot(values[s], grad_masked, 1, 1).reshape(split)
        row_dot = jnp.sum(attention * grad_attention, axis=1, keepdims=True)
        grad_scores = (attention * (grad_attention - row_dot)).astype(BF)
        grad_queries = dot(grad_scores.reshape(GROUP * SRC, TGT), keys[s], 0, 0)
        gq_ref[s] = (grad_queries * scaling).astype(BF)
        grad_keys = [
            (dot(grad_scores[h], head(q, h), 1, 0) * scaling).astype(BF) for h in range(GROUP)
        ]
        grad_values = [
            dot(attention_bf[h], head(grad_masked, h), 1, 0).astype(BF) for h in range(GROUP)
        ]
        grads.append((grad_keys, grad_values))
    for s in range(2):
        slot = slice(s * SRC, (s + 1) * SRC)
        for p in range(GROUP // 2):
            for start, grad in zip((0, HEAD), grads[s]):
                low, high = grad[2 * p], grad[2 * p + 1]
                gkv_ref[p, slot, start : start + HEAD] = jnp.where(swapped, high, low)
                start += 2 * HEAD
                gkv_ref[p, slot, start : start + HEAD] = jnp.where(swapped, low, high)


def partial_kernel(distances, place_ref, grads_ref, own_ref, other_ref, *refs):
    outs, grads = refs[:-1], refs[-1]
    width = SIDE * ROWS

    @pl.when(pl.program_id(0) == 0)
    def _():
        for i, first in enumerate(distances):
            for second in range(SIDE):
                start = (i * SIDE + second) * ROWS
                grads[start : start + ROWS] = grads_ref[chip_at(place_ref, first, second)]

    total = dot(grads[:, : 2 * HEAD], own_ref[...], 1, 1)
    total += dot(grads[:, 2 * HEAD :], other_ref[...], 1, 1)
    for i, out in enumerate(outs):
        out[...] = total[i * width : (i + 1) * width].astype(BF)


def weight_kernel(place_ref, grads_ref, *refs):
    blocks, (own_ref, other_ref, grads) = refs[:SIDE], refs[SIDE:]

    @pl.when(pl.program_id(0) == 0)
    def _():
        for i, second in enumerate(LINE):
            for first in range(SIDE):
                start = (i * SIDE + first) * ROWS
                grads[start : start + ROWS] = grads_ref[chip_at(place_ref, first, second)]

    rows = jnp.concatenate([ref[...] for ref in blocks], axis=0)
    total = dot(rows, grads[...], 0, 0).astype(BF)
    own_ref[...] = total[:, : 2 * HEAD]
    other_ref[...] = total[:, 2 * HEAD :]


def give_back_kernel(rank_ref, grads_ref, *outs):
    for d, out in zip(FAR_FIRST, outs):
        first = jnp.where(rank_ref[d][:1, :1] < 0.5, 1.0, 0.0).astype(BF)
        out[...] = jnp.where(first > 0.5, grads_ref[:SRC], grads_ref[SRC:])


def pick_kernel(place_ref, *refs):
    candidates, out_ref = refs[:PLANES], refs[PLANES]
    for d, ref in zip(FAR_FIRST, candidates):

        @pl.when(place_ref[3] == d)
        def _():
            out_ref[...] = ref[...]


def local(memory, lang_id, src_len, tgt_len, queries, key_weight, value_weight, grad_context):
    plane, y, x = lax.axis_index("lang"), lax.axis_index("y"), lax.axis_index("x")
    core = lax.axis_index("core")
    ahead = jnp.where(core == 0, lang_id[0] - plane, plane - lang_id[0])
    ahead = lax.rem(ahead + PLANES, PLANES)
    place = jnp.stack([plane, y, x, ahead, core]).astype(jnp.int32)

    with jax.named_scope("sentences_over_lang"):
        lane = lax.broadcasted_iota(jnp.int32, (SRC, HEAD), 1)
        numbers = jnp.where(lane == 0, lang_id[0], jnp.where(lane == 1, src_len[0], tgt_len[0]))
        sentence = jnp.concatenate([memory[0], numbers.astype(BF)], axis=1)

    with jax.named_scope("weights_of_chip"):
        key_own, value_own, _ = lax.optimization_barrier((key_weight[0], value_weight[0], sentence))
        own_weight = jnp.concatenate([key_own, value_own], axis=1)
        other_weight = exchange(own_weight)

    with jax.named_scope("sentences_over_lang"):
        late, other_weight = lax.optimization_barrier((sentence, other_weight))
        column = [sentence] + [shift_lang(sentence, d) for d in FAR_FIRST[1:5]]
        column += [shift_lang(late, d) for d in FAR_FIRST[5:]]

    with jax.named_scope("route"):
        routed, rank, lens = pl.pallas_call(
            route_kernel,
            out_shape=(
                jax.ShapeDtypeStruct((ROWS, WIDTH), BF),
                jax.ShapeDtypeStruct((PLANES, 8, HEAD), F32),
                jax.ShapeDtypeStruct((4, 8, HEAD), F32),
            ),
            in_specs=[SMEM] + [VMEM] * PLANES,
            out_specs=(VMEM,) * 3,
            compiler_params=params(16),
        )(place, *column)

    with jax.named_scope("gather_rows"):
        line = pl.pallas_call(
            join_kernel,
            out_shape=jax.ShapeDtypeStruct((SIDE * ROWS, WIDTH), BF),
            in_specs=[ANY] * SIDE,
            out_specs=ANY,
            scratch_shapes=[pltpu.SemaphoreType.DMA((SIDE,))],
            compiler_params=params(1),
        )(routed, *[shift_plane(routed, 0, d) for d in LINE[1:]])
        blocks = [line] + [shift_plane(line, 1, d) for d in LINE[1:]]

    with jax.named_scope("project"):
        projected = pl.pallas_call(
            project_kernel,
            out_shape=jax.ShapeDtypeStruct((CHIPS, ROWS, 4 * HEAD), BF),
            in_specs=[SMEM] + [ANY] * (SIDE + 2),
            out_specs=VMEM,
            scratch_shapes=[
                pltpu.VMEM((SIDE, CHIPS * ROWS, WIDTH // SIDE), BF),
                pltpu.VMEM((SIDE, 2, WIDTH // SIDE, 2 * HEAD), BF),
                pltpu.VMEM((CHIPS * ROWS, 4 * HEAD), F32),
                pltpu.SemaphoreType.DMA((SIDE, 2 + SIDE)),
            ],
            compiler_params=params(40),
        )(place, *blocks, own_weight, other_weight)

    with jax.named_scope("rows_to_slots"):
        slot_rows = lax.all_to_all(projected, PLANE, 0, 0, tiled=True)

    with jax.named_scope("attend"):
        groups = WIDTH // (GROUP * HEAD)
        wide = pl.BlockSpec((2, TGT, GROUP * HEAD), lambda g: (0, 0, g))
        narrow = pl.BlockSpec((GROUP // 2, ROWS, 4 * HEAD), lambda g: (g, 0, 0))
        context, grad_queries, slot_grads = pl.pallas_call(
            attend_kernel,
            grid=(groups,),
            out_shape=(
                jax.ShapeDtypeStruct((2, TGT, WIDTH), BF),
                jax.ShapeDtypeStruct((2, TGT, WIDTH), BF),
                jax.ShapeDtypeStruct((CHIPS, ROWS, 4 * HEAD), BF),
            ),
            in_specs=[SMEM, VMEM, wide, wide, narrow],
            out_specs=(wide, wide, narrow),
            scratch_shapes=[
                pltpu.VMEM((2, GROUP * SRC, GROUP * HEAD), BF),
                pltpu.VMEM((2, GROUP * SRC, GROUP * HEAD), BF),
            ],
            compiler_params=params(58),
        )(place, lens, queries[0], grad_context[0], slot_rows)

    with jax.named_scope("grads_to_heads"):
        head_grads = lax.all_to_all(slot_grads, PLANE, 0, 0, tiled=True)

    with jax.named_scope("sum_rows"):
        tile = WIDTH // SIDE
        terms = {}
        for distances in ((2, 1), (3, 0)):
            count = len(distances)
            found = pl.pallas_call(
                functools.partial(partial_kernel, distances),
                grid=(WIDTH // tile,),
                out_shape=(jax.ShapeDtypeStruct((SIDE * ROWS, WIDTH), BF),) * count,
                in_specs=[SMEM, VMEM] + [pl.BlockSpec((tile, 2 * HEAD), lambda t: (t, 0))] * 2,
                out_specs=(pl.BlockSpec((SIDE * ROWS, tile), lambda t: (0, t)),) * count,
                scratch_shapes=[pltpu.VMEM((count * SIDE * ROWS, 4 * HEAD), BF)],
                compiler_params=params(24),
                cost_estimate=cost(count * SIDE * ROWS * WIDTH * 4 * HEAD, 7),
            )(place, head_grads, own_weight, other_weight)
            terms.update(zip(distances, found))
        arrived = [terms[0]] + [shift_plane(terms[d], 0, -d) for d in LINE[1:]]
        line = sum(term.astype(F32) for term in arrived).astype(BF)

    with jax.named_scope("weight_grads"):
        head_grads, _ = lax.optimization_barrier((head_grads, terms))
        tile = WIDTH // 8
        keep, send = pl.pallas_call(
            weight_kernel,
            grid=(WIDTH // tile,),
            out_shape=(jax.ShapeDtypeStruct((WIDTH, 2 * HEAD), BF),) * 2,
            in_specs=[SMEM, VMEM]
            + [pl.BlockSpec((SIDE * ROWS, tile), lambda t: (0, t))] * SIDE,
            out_specs=(pl.BlockSpec((tile, 2 * HEAD), lambda t: (t, 0)),) * 2,
            scratch_shapes=[pltpu.VMEM((CHIPS * ROWS, 4 * HEAD), BF)],
            compiler_params=params(32),
            cost_estimate=cost(CHIPS * ROWS * WIDTH * 4 * HEAD, 16),
        )(place, head_grads, *blocks)
        both = exchange(send)
        weight_grads = [
            (keep[:, cols].astype(F32) + both[:, cols].astype(F32)).astype(BF)
            for cols in (slice(0, HEAD), slice(HEAD, 2 * HEAD))
        ]

    with jax.named_scope("sum_rows"):
        pieces = {d: line[d * ROWS : (d + 1) * ROWS] for d in LINE}
        arrived = [pieces[0]] + [shift_plane(pieces[d], 1, -d) for d in LINE[1:]]
        summed = sum(term.astype(F32) for term in arrived).astype(BF)

    with jax.named_scope("sentences_back"):
        sends = pl.pallas_call(
            give_back_kernel,
            out_shape=(jax.ShapeDtypeStruct((SRC, WIDTH), BF),) * PLANES,
            in_specs=[VMEM] * 2,
            out_specs=(VMEM,) * PLANES,
            compiler_params=params(16),
        )(rank, summed)
        late, weight_grads = lax.optimization_barrier((sends[5:], weight_grads))
        sends = [*sends[:5], *late]
        candidates = [sends[0]] + [shift_lang(sends[i], -FAR_FIRST[i]) for i in range(1, PLANES)]
        grad_memory = pl.pallas_call(
            pick_kernel,
            out_shape=jax.ShapeDtypeStruct((SRC, WIDTH), BF),
            in_specs=[SMEM] + [VMEM] * PLANES,
            out_specs=VMEM,
            compiler_params=params(16),
        )(place, *candidates)

    return (
        context[None],
        grad_queries[None],
        grad_memory[None],
        weight_grads[0][None],
        weight_grads[1][None],
    )


def solution(mesh):
    planes = mesh.shape["lang"]
    grid = Mesh(mesh.devices.reshape(planes, SIDE, SIDE, 2), ("lang", "y", "x", "core"))
    shard = ("y", "x", "core")
    every = ("lang", "y", "x", "core")
    return jax.shard_map(
        local,
        mesh=grid,
        in_specs=(
            P(every, None, None),
            P(every),
            P(every),
            P(every),
            P("lang", shard, None, None),
            P("lang", None, shard),
            P("lang", None, shard),
            P("lang", shard, None, None),
        ),
        out_specs=(
            P("lang", shard, None, None),
            P("lang", shard, None, None),
            P(every, None, None),
            P("lang", None, shard),
            P("lang", None, shard),
        ),
        check_vma=False,
    )
```

```python
import functools

import jax
import jax.numpy as jnp
from jax import lax
from jax.experimental import pallas as pl
from jax.experimental.pallas import tpu as pltpu
from jax.sharding import Mesh, PartitionSpec as P

HEAD = 128
SRC = 16
TGT = 128
WIDTH = 4096
PLANES = 8
SIDE = 4
CHIPS = SIDE * SIDE
ROWS = 32
GROUP = 8
MASKED = -1e30
BF = jnp.bfloat16
F32 = jnp.float32
PLANE = ("y", "x")
FAR_FIRST = (0, 4, 3, 5, 2, 6, 1, 7)
NEAR_FIRST = (0, 7, 1, 6, 2, 5, 3, 4)
LINE = (0, 2, 1, 3)
EARLY, LATE = (0, 3), (1, 2)
VMEM = pl.BlockSpec(memory_space=pltpu.VMEM)
SMEM = pl.BlockSpec(memory_space=pltpu.SMEM)
ANY = pl.BlockSpec(memory_space=pl.ANY)


def params(mib):
    return pltpu.CompilerParams(vmem_limit_bytes=mib << 20)


def cost(products, mib):
    return pl.CostEstimate(flops=2 * products, bytes_accessed=mib << 20, transcendentals=0)


def exchange(value):
    return lax.ppermute(value, "core", [(0, 1), (1, 0)])


def shift_lang(value, step):
    pairs = [
        (2 * z + c, 2 * ((z + (step if c == 0 else -step)) % PLANES) + c)
        for z in range(PLANES)
        for c in range(2)
    ]
    return lax.ppermute(value, ("lang", "core"), pairs)


def shift_plane(value, phase, step):
    pairs = []
    for y in range(SIDE):
        for x in range(SIDE):
            for c in range(2):
                along_x = c == phase
                to_y = y if along_x else (y + step) % SIDE
                to_x = (x + step) % SIDE if along_x else x
                pairs.append(((y * SIDE + x) * 2 + c, (to_y * SIDE + to_x) * 2 + c))
    return lax.ppermute(value, ("y", "x", "core"), pairs)


def dot(a, b, ca, cb):
    return lax.dot_general(a, b, (((ca,), (cb,)), ((), ())), preferred_element_type=F32)


def chip_at(place_ref, first, second):
    y, x, core = place_ref[1], place_ref[2], place_ref[4]
    dy = jnp.where(core == 0, second, first)
    dx = jnp.where(core == 0, first, second)
    return lax.rem(y - dy + SIDE, SIDE) * SIDE + lax.rem(x - dx + SIDE, SIDE)


def route_kernel(place_ref, *refs):
    sentences, (routed_ref, rank_ref, lens_ref) = refs[:PLANES], refs[PLANES:]
    sentences = [sentences[NEAR_FIRST.index(d)] for d in range(PLANES)]
    plane, core = place_ref[0], place_ref[4]
    plane_f = plane.astype(F32)
    match, rank = [], []
    for ref in sentences:
        lang = ref[:, WIDTH : WIDTH + 1].astype(F32)
        match.append(jnp.where(lang == plane_f, 1.0, 0.0))
    origin = [
        lax.rem(plane + jnp.where(core == 0, PLANES - d, d), PLANES) for d in range(PLANES)
    ]
    for d in range(PLANES):
        before = jnp.zeros((SRC, 1), F32)
        for e in range(PLANES):
            if e != d:
                before += jnp.where(origin[e] < origin[d], match[e], 0.0)
        rank.append(jnp.where(match[d] > 0.5, before, -1.0))
        rank_ref[d] = jnp.broadcast_to(rank[d][:8], (8, HEAD))
    for r in range(2):
        src = jnp.zeros((8, 1), F32)
        tgt = jnp.zeros((8, 1), F32)
        total = jnp.zeros((SRC, WIDTH), BF)
        for d, ref in enumerate(sentences):
            here = rank[d] == float(r)
            src = jnp.where(here[:8], ref[:8, WIDTH + 1 : WIDTH + 2].astype(F32), src)
            tgt = jnp.where(here[:8], ref[:8, WIDTH + 2 : WIDTH + 3].astype(F32), tgt)
            wide = jnp.where(here, 1.0, 0.0).astype(BF)
            total = jnp.where(wide > 0.5, ref[:, :WIDTH], total)
        lens_ref[r] = jnp.broadcast_to(src, (8, HEAD))
        lens_ref[2 + r] = jnp.broadcast_to(tgt, (8, HEAD))
        routed_ref[r * SRC : (r + 1) * SRC] = total


def join_kernel(*refs):
    parts, out, sems = refs[:SIDE], refs[SIDE], refs[SIDE + 1]
    copies = [
        pltpu.make_async_copy(part, out.at[pl.ds(d * ROWS, ROWS)], sems.at[i])
        for i, (part, d) in enumerate(zip(parts, LINE))
    ]
    for copy in copies:
        copy.start()
    for copy in copies:
        copy.wait()


def project_kernel(distances, place_ref, *refs):
    count = len(distances)
    blocks, weights, out_ref = refs[:count], refs[count : count + 4], refs[count + 4]
    rows, weight, part, sems = refs[count + 5 :]
    step = WIDTH // SIDE
    copies = []
    for k in range(SIDE):
        span = pl.ds(k * step, step)
        chunk = []
        for i, ref in enumerate(weights):
            into = weight.at[k, i // 2, :, pl.ds(i % 2 * HEAD, HEAD)]
            chunk.append(pltpu.make_async_copy(ref.at[span], into, sems.at[k, i]))
        for i, ref in enumerate(blocks):
            into = rows.at[k, pl.ds(i * SIDE * ROWS, SIDE * ROWS)]
            chunk.append(pltpu.make_async_copy(ref.at[:, span], into, sems.at[k, 4 + i]))
        copies.append(chunk)
        for copy in chunk:
            copy.start()
    for k, chunk in enumerate(copies):
        for copy in chunk:
            copy.wait()
        for i in range(2):
            cols = slice(i * 2 * HEAD, (i + 1) * 2 * HEAD)
            term = dot(rows[k], weight[k, i], 1, 0)
            part[:, cols] = term if k == 0 else part[:, cols] + term
    out_ref[...] = part[...].astype(BF)


def project_rest_kernel(distances, place_ref, early_ref, *refs):
    count = len(distances) + 4
    out_ref, late = refs[count], refs[-1]
    project_kernel(distances, place_ref, *refs[:count], late, *refs[count + 1 : -1])
    for found, seconds in ((early_ref, EARLY), (late, distances)):
        for i, second in enumerate(seconds):
            for first in range(SIDE):
                start = (i * SIDE + first) * ROWS
                out_ref[chip_at(place_ref, first, second)] = found[start : start + ROWS]


def head(array, h):
    return array[:, h * HEAD : (h + 1) * HEAD]


def lay_out(place_ref, kv_ref, keys, values):
    swapped = place_ref[4] == 1

    @pl.when(pl.program_id(0) == 0)
    def _():
        keys[...] = jnp.zeros_like(keys)
        values[...] = jnp.zeros_like(values)

    for s in range(2):
        slot = slice(s * SRC, (s + 1) * SRC)
        for h in range(GROUP):
            rows, cols = slice(h * SRC, (h + 1) * SRC), slice(h * HEAD, (h + 1) * HEAD)
            own, other = (h % 2) * 2 * HEAD, (1 - h % 2) * 2 * HEAD
            for start, block in ((0, keys), (HEAD, values)):
                block[s, rows, cols] = jnp.where(
                    swapped,
                    kv_ref[h // 2, slot, other + start : other + start + HEAD],
                    kv_ref[h // 2, slot, own + start : own + start + HEAD],
                )


def valid_rows(lens_ref, s):
    row_index = lax.broadcasted_iota(jnp.int32, (TGT, 1), 0).astype(F32)
    return row_index < lens_ref[2 + s][:1, :1]


def attend_kernel(
    place_ref, lens_ref, q_ref, g_ref, kv_ref, gkv_ref, attention_ref, grad_scores_ref, keys, values
):
    swapped = place_ref[4] == 1
    scaling = HEAD ** (-0.5)
    split = (GROUP, SRC, TGT)
    lay_out(place_ref, kv_ref, keys, values)
    grads = []
    for s in range(2):
        src = jnp.maximum(lens_ref[s][:1], 1.0)[None]
        q, g = q_ref[s], g_ref[s]
        valid = jnp.where(valid_rows(lens_ref, s), 1.0, 0.0).astype(BF)
        grad_masked = jnp.where(valid > 0.5, g, jnp.zeros_like(g))
        scores = (dot(keys[s], q, 1, 1) * scaling).reshape(split)
        key_index = lax.broadcasted_iota(jnp.int32, split, 1).astype(F32)
        scores = jnp.where(key_index < src, scores, MASKED)
        shifted = jnp.exp(scores - jnp.max(scores, axis=1, keepdims=True))
        attention = shifted / jnp.sum(shifted, axis=1, keepdims=True)
        attention_bf = attention.astype(BF)
        attention_ref[s] = attention_bf.reshape(GROUP * SRC, TGT)
        grad_attention = dot(values[s], grad_masked, 1, 1).reshape(split)
        row_dot = jnp.sum(attention * grad_attention, axis=1, keepdims=True)
        grad_scores = (attention * (grad_attention - row_dot)).astype(BF)
        grad_scores_ref[s] = grad_scores.reshape(GROUP * SRC, TGT)
        grad_keys = [
            (dot(grad_scores[h], head(q, h), 1, 0) * scaling).astype(BF) for h in range(GROUP)
        ]
        grad_values = [
            dot(attention_bf[h], head(grad_masked, h), 1, 0).astype(BF) for h in range(GROUP)
        ]
        grads.append((grad_keys, grad_values))
    for s in range(2):
        slot = slice(s * SRC, (s + 1) * SRC)
        for p in range(GROUP // 2):
            for start, grad in zip((0, HEAD), grads[s]):
                low, high = grad[2 * p], grad[2 * p + 1]
                gkv_ref[p, slot, start : start + HEAD] = jnp.where(swapped, high, low)
                start += 2 * HEAD
                gkv_ref[p, slot, start : start + HEAD] = jnp.where(swapped, low, high)


def outputs_kernel(
    place_ref, lens_ref, attention_ref, grad_scores_ref, kv_ref, ctx_ref, gq_ref, keys, values
):
    scaling = HEAD ** (-0.5)
    lay_out(place_ref, kv_ref, keys, values)
    for s in range(2):
        context = dot(attention_ref[s], values[s], 0, 0)
        ctx_ref[s] = jnp.where(valid_rows(lens_ref, s), context, 0.0).astype(BF)
        gq_ref[s] = (dot(grad_scores_ref[s], keys[s], 0, 0) * scaling).astype(BF)


def partial_kernel(distances, place_ref, grads_ref, *refs):
    weights, outs, grads = refs[:4], refs[4:-1], refs[-1]
    width = SIDE * ROWS

    @pl.when(pl.program_id(0) == 0)
    def _():
        for i, first in enumerate(distances):
            for second in range(SIDE):
                start = (i * SIDE + second) * ROWS
                grads[start : start + ROWS] = grads_ref[chip_at(place_ref, first, second)]

    own, other = (jnp.concatenate([weights[i][...], weights[i + 1][...]], axis=1) for i in (0, 2))
    total = dot(grads[:, : 2 * HEAD], own, 1, 1)
    total += dot(grads[:, 2 * HEAD :], other, 1, 1)
    for i, out in enumerate(outs):
        out[...] = total[i * width : (i + 1) * width].astype(BF)


def weight_kernel(place_ref, grads_ref, *refs):
    blocks, (own_ref, other_ref, grads) = refs[:SIDE], refs[SIDE:]

    @pl.when(pl.program_id(0) == 0)
    def _():
        for i, second in enumerate(LINE):
            for first in range(SIDE):
                start = (i * SIDE + first) * ROWS
                grads[start : start + ROWS] = grads_ref[chip_at(place_ref, first, second)]

    rows = jnp.concatenate([ref[...] for ref in blocks], axis=0)
    total = dot(rows, grads[...], 0, 0).astype(BF)
    own_ref[...] = total[:, : 2 * HEAD]
    other_ref[...] = total[:, 2 * HEAD :]


def give_back_kernel(rank_ref, grads_ref, *outs):
    for d, out in zip(FAR_FIRST, outs):
        first = jnp.where(rank_ref[d][:1, :1] < 0.5, 1.0, 0.0).astype(BF)
        out[...] = jnp.where(first > 0.5, grads_ref[:SRC], grads_ref[SRC:])


def pick_kernel(place_ref, *refs):
    candidates, out_ref = refs[:PLANES], refs[PLANES]
    for d, ref in zip(FAR_FIRST, candidates):

        @pl.when(place_ref[3] == d)
        def _():
            out_ref[...] = ref[...]


def local(memory, lang_id, src_len, tgt_len, queries, key_weight, value_weight, grad_context):
    plane, y, x = lax.axis_index("lang"), lax.axis_index("y"), lax.axis_index("x")
    core = lax.axis_index("core")
    ahead = jnp.where(core == 0, lang_id[0] - plane, plane - lang_id[0])
    ahead = lax.rem(ahead + PLANES, PLANES)
    place = jnp.stack([plane, y, x, ahead, core]).astype(jnp.int32)

    with jax.named_scope("sentences_over_lang"):
        lane = lax.broadcasted_iota(jnp.int32, (SRC, HEAD), 1)
        numbers = jnp.where(lane == 0, lang_id[0], jnp.where(lane == 1, src_len[0], tgt_len[0]))
        sentence = jnp.concatenate([memory[0], numbers.astype(BF)], axis=1)

        column = [sentence] + [shift_lang(sentence, d) for d in FAR_FIRST[1:]]

    with jax.named_scope("route"):
        routed, rank, lens = pl.pallas_call(
            route_kernel,
            out_shape=(
                jax.ShapeDtypeStruct((ROWS, WIDTH), BF),
                jax.ShapeDtypeStruct((PLANES, 8, HEAD), F32),
                jax.ShapeDtypeStruct((4, 8, HEAD), F32),
            ),
            in_specs=[SMEM] + [VMEM] * PLANES,
            out_specs=(VMEM,) * 3,
            compiler_params=params(16),
        )(place, *[column[FAR_FIRST.index(d)] for d in NEAR_FIRST])

    with jax.named_scope("weights_of_chip"):
        key_own, value_own, routed = lax.optimization_barrier(
            (key_weight[0], value_weight[0], routed)
        )
        weights = (key_own, value_own, exchange(key_own), exchange(value_own))

    with jax.named_scope("gather_rows"):
        line = pl.pallas_call(
            join_kernel,
            out_shape=jax.ShapeDtypeStruct((SIDE * ROWS, WIDTH), BF),
            in_specs=[ANY] * SIDE,
            out_specs=ANY,
            scratch_shapes=[pltpu.SemaphoreType.DMA((SIDE,))],
            compiler_params=params(1),
        )(routed, *[shift_plane(routed, 0, d) for d in LINE[1:]])
        blocks = [line] + [shift_plane(line, 1, d) for d in LINE[1:]]

    with jax.named_scope("project"):
        count = SIDE // 2
        scratch = [
            pltpu.VMEM((SIDE, count * SIDE * ROWS, WIDTH // SIDE), BF),
            pltpu.VMEM((SIDE, 2, WIDTH // SIDE, 2 * HEAD), BF),
            pltpu.VMEM((count * SIDE * ROWS, 4 * HEAD), F32),
            pltpu.SemaphoreType.DMA((SIDE, 4 + count)),
        ]
        block_at = dict(zip(LINE, blocks))
        early = pl.pallas_call(
            functools.partial(project_kernel, EARLY),
            out_shape=jax.ShapeDtypeStruct((count * SIDE * ROWS, 4 * HEAD), BF),
            in_specs=[SMEM] + [ANY] * (count + 4),
            out_specs=VMEM,
            scratch_shapes=scratch,
            compiler_params=params(24),
            cost_estimate=cost(count * SIDE * ROWS * WIDTH * 4 * HEAD, 6),
        )(place, *[block_at[d] for d in EARLY], *weights)
        projected = pl.pallas_call(
            functools.partial(project_rest_kernel, LATE),
            out_shape=jax.ShapeDtypeStruct((CHIPS, ROWS, 4 * HEAD), BF),
            in_specs=[SMEM, VMEM] + [ANY] * (count + 4),
            out_specs=VMEM,
            scratch_shapes=scratch + [pltpu.VMEM((count * SIDE * ROWS, 4 * HEAD), BF)],
            compiler_params=params(24),
            cost_estimate=cost(count * SIDE * ROWS * WIDTH * 4 * HEAD, 6),
        )(place, early, *[block_at[d] for d in LATE], *weights)

    with jax.named_scope("rows_to_slots"):
        slot_rows = lax.all_to_all(projected, PLANE, 0, 0, tiled=True)

    with jax.named_scope("attend"):
        groups = WIDTH // (GROUP * HEAD)
        wide = pl.BlockSpec((2, TGT, GROUP * HEAD), lambda g: (0, 0, g))
        narrow = pl.BlockSpec((GROUP // 2, ROWS, 4 * HEAD), lambda g: (g, 0, 0))
        tall = pl.BlockSpec((2, GROUP * SRC, TGT), lambda g: (0, g, 0))
        diagonal = [pltpu.VMEM((2, GROUP * SRC, GROUP * HEAD), BF)] * 2
        slot_grads, attention, grad_scores = pl.pallas_call(
            attend_kernel,
            grid=(groups,),
            out_shape=(jax.ShapeDtypeStruct((CHIPS, ROWS, 4 * HEAD), BF),)
            + (jax.ShapeDtypeStruct((2, groups * GROUP * SRC, TGT), BF),) * 2,
            in_specs=[SMEM, VMEM, wide, wide, narrow],
            out_specs=(narrow, tall, tall),
            scratch_shapes=diagonal,
            compiler_params=params(58),
            cost_estimate=cost(1 << 29, 6),
        )(place, lens, queries[0], grad_context[0], slot_rows)

    with jax.named_scope("grads_to_heads"):
        head_grads = lax.all_to_all(slot_grads, PLANE, 0, 0, tiled=True)

    with jax.named_scope("attend"):
        context, grad_queries = pl.pallas_call(
            outputs_kernel,
            grid=(groups,),
            out_shape=(jax.ShapeDtypeStruct((2, TGT, WIDTH), BF),) * 2,
            in_specs=[SMEM, VMEM, tall, tall, narrow],
            out_specs=(wide, wide),
            scratch_shapes=diagonal,
            compiler_params=params(32),
            cost_estimate=cost(1 << 30, 16),
        )(place, lens, attention, grad_scores, slot_rows)

    with jax.named_scope("sum_rows"):
        tile = WIDTH // SIDE
        terms = {}
        for distances in ((2, 1), (3, 0)):
            count = len(distances)
            found = pl.pallas_call(
                functools.partial(partial_kernel, distances),
                grid=(WIDTH // tile,),
                out_shape=(jax.ShapeDtypeStruct((SIDE * ROWS, WIDTH), BF),) * count,
                in_specs=[SMEM, VMEM] + [pl.BlockSpec((tile, HEAD), lambda t: (t, 0))] * 4,
                out_specs=(pl.BlockSpec((SIDE * ROWS, tile), lambda t: (0, t)),) * count,
                scratch_shapes=[pltpu.VMEM((count * SIDE * ROWS, 4 * HEAD), BF)],
                compiler_params=params(24),
                cost_estimate=cost(count * SIDE * ROWS * WIDTH * 4 * HEAD, 7),
            )(place, head_grads, *weights)
            terms.update(zip(distances, found))
        arrived = [terms[0]] + [shift_plane(terms[d], 0, -d) for d in LINE[1:]]
        arrived[1], context, grad_queries = lax.optimization_barrier(
            (arrived[1], context, grad_queries)
        )
        line = sum(term.astype(F32) for term in arrived).astype(BF)

    with jax.named_scope("weight_grads"):
        head_grads, _ = lax.optimization_barrier((head_grads, terms))
        tile = WIDTH // 8
        keep, send = pl.pallas_call(
            weight_kernel,
            grid=(WIDTH // tile,),
            out_shape=(jax.ShapeDtypeStruct((WIDTH, 2 * HEAD), BF),) * 2,
            in_specs=[SMEM, VMEM]
            + [pl.BlockSpec((SIDE * ROWS, tile), lambda t: (0, t))] * SIDE,
            out_specs=(pl.BlockSpec((tile, 2 * HEAD), lambda t: (t, 0)),) * 2,
            scratch_shapes=[pltpu.VMEM((CHIPS * ROWS, 4 * HEAD), BF)],
            compiler_params=params(32),
            cost_estimate=cost(CHIPS * ROWS * WIDTH * 4 * HEAD, 16),
        )(place, head_grads, *blocks)
        both = exchange(send)
        weight_grads = [
            (keep[:, cols].astype(F32) + both[:, cols].astype(F32)).astype(BF)
            for cols in (slice(0, HEAD), slice(HEAD, 2 * HEAD))
        ]

    with jax.named_scope("sum_rows"):
        pieces = {d: line[d * ROWS : (d + 1) * ROWS] for d in LINE}
        arrived = [pieces[0]] + [shift_plane(pieces[d], 1, -d) for d in LINE[1:]]
        arrived[1], weight_grads = lax.optimization_barrier((arrived[1], weight_grads))
        summed = sum(term.astype(F32) for term in arrived).astype(BF)

    with jax.named_scope("sentences_back"):
        sends = pl.pallas_call(
            give_back_kernel,
            out_shape=(jax.ShapeDtypeStruct((SRC, WIDTH), BF),) * PLANES,
            in_specs=[VMEM] * 2,
            out_specs=(VMEM,) * PLANES,
            compiler_params=params(16),
        )(rank, summed)
        candidates = [sends[0]] + [shift_lang(sends[i], -FAR_FIRST[i]) for i in range(1, PLANES)]
        grad_memory = pl.pallas_call(
            pick_kernel,
            out_shape=jax.ShapeDtypeStruct((SRC, WIDTH), BF),
            in_specs=[SMEM] + [VMEM] * PLANES,
            out_specs=VMEM,
            compiler_params=params(16),
        )(place, *candidates)

    return (
        context[None],
        grad_queries[None],
        grad_memory[None],
        weight_grads[0][None],
        weight_grads[1][None],
    )


def solution(mesh):
    planes = mesh.shape["lang"]
    grid = Mesh(mesh.devices.reshape(planes, SIDE, SIDE, 2), ("lang", "y", "x", "core"))
    shard = ("y", "x", "core")
    every = ("lang", "y", "x", "core")
    return jax.shard_map(
        local,
        mesh=grid,
        in_specs=(
            P(every, None, None),
            P(every),
            P(every),
            P(every),
            P("lang", shard, None, None),
            P("lang", None, shard),
            P("lang", None, shard),
            P("lang", shard, None, None),
        ),
        out_specs=(
            P("lang", shard, None, None),
            P("lang", shard, None, None),
            P(every, None, None),
            P("lang", None, shard),
            P("lang", None, shard),
        ),
        check_vma=False,
    )
```

```python
import functools

import jax
import jax.numpy as jnp
from jax import lax
from jax.experimental import pallas as pl
from jax.experimental.pallas import tpu as pltpu
from jax.sharding import Mesh, PartitionSpec as P

HEAD = 128
SRC = 16
TGT = 128
WIDTH = 4096
PLANES = 8
SIDE = 4
CHIPS = SIDE * SIDE
ROWS = 32
GROUP = 8
MASKED = -1e30
BF = jnp.bfloat16
F32 = jnp.float32
PLANE = ("y", "x")
FAR_FIRST = (0, 4, 3, 5, 2, 6, 1, 7)
NEAR_FIRST = (0, 7, 1, 6, 2, 5, 3, 4)
LINE = (0, 2, 1, 3)
EARLY, LATE = (0, 3), (1, 2)
VMEM = pl.BlockSpec(memory_space=pltpu.VMEM)
SMEM = pl.BlockSpec(memory_space=pltpu.SMEM)
ANY = pl.BlockSpec(memory_space=pl.ANY)


def params(mib):
    return pltpu.CompilerParams(vmem_limit_bytes=mib << 20)


def cost(products, mib):
    return pl.CostEstimate(flops=2 * products, bytes_accessed=mib << 20, transcendentals=0)


def exchange(value):
    return lax.ppermute(value, "core", [(0, 1), (1, 0)])


def shift_lang(value, step):
    pairs = [
        (2 * z + c, 2 * ((z + (step if c == 0 else -step)) % PLANES) + c)
        for z in range(PLANES)
        for c in range(2)
    ]
    return lax.ppermute(value, ("lang", "core"), pairs)


def shift_plane(value, phase, step):
    pairs = []
    for y in range(SIDE):
        for x in range(SIDE):
            for c in range(2):
                along_x = c == phase
                to_y = y if along_x else (y + step) % SIDE
                to_x = (x + step) % SIDE if along_x else x
                pairs.append(((y * SIDE + x) * 2 + c, (to_y * SIDE + to_x) * 2 + c))
    return lax.ppermute(value, ("y", "x", "core"), pairs)


def dot(a, b, ca, cb):
    return lax.dot_general(a, b, (((ca,), (cb,)), ((), ())), preferred_element_type=F32)


def chip_at(place_ref, first, second):
    y, x, core = place_ref[1], place_ref[2], place_ref[4]
    dy = jnp.where(core == 0, second, first)
    dx = jnp.where(core == 0, first, second)
    return lax.rem(y - dy + SIDE, SIDE) * SIDE + lax.rem(x - dx + SIDE, SIDE)


def label_kernel(memory_ref, lang_ref, src_ref, tgt_ref, out_ref):
    lane = lax.broadcasted_iota(jnp.int32, (SRC, HEAD), 1)
    numbers = jnp.where(lane == 0, lang_ref[...], jnp.where(lane == 1, src_ref[...], tgt_ref[...]))
    out_ref[:, :WIDTH] = memory_ref[...]
    out_ref[:, WIDTH:] = numbers.astype(F32).astype(BF)


def route_kernel(place_ref, *refs):
    sentences, (routed_ref, rank_ref, lens_ref) = refs[:PLANES], refs[PLANES:]
    sentences = [sentences[NEAR_FIRST.index(d)] for d in range(PLANES)]
    plane, core = place_ref[0], place_ref[4]
    plane_f = plane.astype(F32)
    match, rank = [], []
    for ref in sentences:
        lang = ref[:, WIDTH : WIDTH + 1].astype(F32)
        match.append(jnp.where(lang == plane_f, 1.0, 0.0))
    origin = [
        lax.rem(plane + jnp.where(core == 0, PLANES - d, d), PLANES) for d in range(PLANES)
    ]
    for d in range(PLANES):
        before = jnp.zeros((SRC, 1), F32)
        for e in range(PLANES):
            if e != d:
                before += jnp.where(origin[e] < origin[d], match[e], 0.0)
        rank.append(jnp.where(match[d] > 0.5, before, -1.0))
        rank_ref[d] = jnp.broadcast_to(rank[d][:8], (8, HEAD))
    for r in range(2):
        src = jnp.zeros((8, 1), F32)
        tgt = jnp.zeros((8, 1), F32)
        total = jnp.zeros((SRC, WIDTH), BF)
        for d, ref in enumerate(sentences):
            here = rank[d] == float(r)
            src = jnp.where(here[:8], ref[:8, WIDTH + 1 : WIDTH + 2].astype(F32), src)
            tgt = jnp.where(here[:8], ref[:8, WIDTH + 2 : WIDTH + 3].astype(F32), tgt)
            wide = jnp.where(here, 1.0, 0.0).astype(BF)
            total = jnp.where(wide > 0.5, ref[:, :WIDTH], total)
        lens_ref[r] = jnp.broadcast_to(src, (8, HEAD))
        lens_ref[2 + r] = jnp.broadcast_to(tgt, (8, HEAD))
        routed_ref[r * SRC : (r + 1) * SRC] = total


def join_kernel(*refs):
    parts, out, sems = refs[:SIDE], refs[SIDE], refs[SIDE + 1]
    copies = [
        pltpu.make_async_copy(part, out.at[pl.ds(d * ROWS, ROWS)], sems.at[i])
        for i, (part, d) in enumerate(zip(parts, LINE))
    ]
    for copy in copies:
        copy.start()
    for copy in copies:
        copy.wait()


def project_kernel(distances, place_ref, *refs):
    count = len(distances)
    blocks, weights, out_ref = refs[:count], refs[count : count + 4], refs[count + 4]
    rows, weight, part, sems = refs[count + 5 :]
    step = WIDTH // SIDE
    copies = []
    for k in range(SIDE):
        span = pl.ds(k * step, step)
        chunk = []
        for i, ref in enumerate(weights):
            into = weight.at[k, i // 2, :, pl.ds(i % 2 * HEAD, HEAD)]
            chunk.append(pltpu.make_async_copy(ref.at[span], into, sems.at[k, i]))
        for i, ref in enumerate(blocks):
            into = rows.at[k, pl.ds(i * SIDE * ROWS, SIDE * ROWS)]
            chunk.append(pltpu.make_async_copy(ref.at[:, span], into, sems.at[k, 4 + i]))
        copies.append(chunk)
        for copy in chunk:
            copy.start()
    for k, chunk in enumerate(copies):
        for copy in chunk:
            copy.wait()
        for i in range(2):
            cols = slice(i * 2 * HEAD, (i + 1) * 2 * HEAD)
            term = dot(rows[k], weight[k, i], 1, 0)
            part[:, cols] = term if k == 0 else part[:, cols] + term
    out_ref[...] = part[...].astype(BF)


def project_rest_kernel(distances, place_ref, early_ref, *refs):
    count = len(distances) + 4
    out_ref, late = refs[count], refs[-1]
    project_kernel(distances, place_ref, *refs[:count], late, *refs[count + 1 : -1])
    for found, seconds in ((early_ref, EARLY), (late, distances)):
        for i, second in enumerate(seconds):
            for first in range(SIDE):
                start = (i * SIDE + first) * ROWS
                out_ref[chip_at(place_ref, first, second)] = found[start : start + ROWS]


def head(array, h):
    return array[:, h * HEAD : (h + 1) * HEAD]


def lay_out(place_ref, kv_ref, keys, values):
    swapped = place_ref[4] == 1

    @pl.when(pl.program_id(0) == 0)
    def _():
        keys[...] = jnp.zeros_like(keys)
        values[...] = jnp.zeros_like(values)

    for s in range(2):
        slot = slice(s * SRC, (s + 1) * SRC)
        for h in range(GROUP):
            rows, cols = slice(h * SRC, (h + 1) * SRC), slice(h * HEAD, (h + 1) * HEAD)
            own, other = (h % 2) * 2 * HEAD, (1 - h % 2) * 2 * HEAD
            for start, block in ((0, keys), (HEAD, values)):
                block[s, rows, cols] = jnp.where(
                    swapped,
                    kv_ref[h // 2, slot, other + start : other + start + HEAD],
                    kv_ref[h // 2, slot, own + start : own + start + HEAD],
                )


def valid_rows(lens_ref, s):
    row_index = lax.broadcasted_iota(jnp.int32, (TGT, 1), 0).astype(F32)
    return row_index < lens_ref[2 + s][:1, :1]


def attend_kernel(
    place_ref, lens_ref, q_ref, g_ref, kv_ref, gkv_ref, attention_ref, grad_scores_ref, keys, values
):
    swapped = place_ref[4] == 1
    scaling = HEAD ** (-0.5)
    split = (GROUP, SRC, TGT)
    lay_out(place_ref, kv_ref, keys, values)
    grads = []
    for s in range(2):
        src = jnp.maximum(lens_ref[s][:1], 1.0)[None]
        q, g = q_ref[s], g_ref[s]
        valid = jnp.where(valid_rows(lens_ref, s), 1.0, 0.0).astype(BF)
        grad_masked = jnp.where(valid > 0.5, g, jnp.zeros_like(g))
        scores = (dot(keys[s], q, 1, 1) * scaling).reshape(split)
        key_index = lax.broadcasted_iota(jnp.int32, split, 1).astype(F32)
        scores = jnp.where(key_index < src, scores, MASKED)
        shifted = jnp.exp(scores - jnp.max(scores, axis=1, keepdims=True))
        attention = shifted / jnp.sum(shifted, axis=1, keepdims=True)
        attention_bf = attention.astype(BF)
        attention_ref[s] = attention_bf.reshape(GROUP * SRC, TGT)
        grad_attention = dot(values[s], grad_masked, 1, 1).reshape(split)
        row_dot = jnp.sum(attention * grad_attention, axis=1, keepdims=True)
        grad_scores = (attention * (grad_attention - row_dot)).astype(BF)
        grad_scores_ref[s] = grad_scores.reshape(GROUP * SRC, TGT)
        grad_keys = [
            (dot(grad_scores[h], head(q, h), 1, 0) * scaling).astype(BF) for h in range(GROUP)
        ]
        grad_values = [
            dot(attention_bf[h], head(grad_masked, h), 1, 0).astype(BF) for h in range(GROUP)
        ]
        grads.append((grad_keys, grad_values))
    for s in range(2):
        slot = slice(s * SRC, (s + 1) * SRC)
        for p in range(GROUP // 2):
            for start, grad in zip((0, HEAD), grads[s]):
                low, high = grad[2 * p], grad[2 * p + 1]
                gkv_ref[p, slot, start : start + HEAD] = jnp.where(swapped, high, low)
                start += 2 * HEAD
                gkv_ref[p, slot, start : start + HEAD] = jnp.where(swapped, low, high)


def outputs_kernel(
    place_ref, lens_ref, attention_ref, grad_scores_ref, kv_ref, ctx_ref, gq_ref, keys, values
):
    scaling = HEAD ** (-0.5)
    lay_out(place_ref, kv_ref, keys, values)
    for s in range(2):
        context = dot(attention_ref[s], values[s], 0, 0)
        ctx_ref[s] = jnp.where(valid_rows(lens_ref, s), context, 0.0).astype(BF)
        gq_ref[s] = (dot(grad_scores_ref[s], keys[s], 0, 0) * scaling).astype(BF)


def partial_kernel(distances, place_ref, grads_ref, *refs):
    weights, outs, grads = refs[:4], refs[4:-1], refs[-1]
    width = SIDE * ROWS

    @pl.when(pl.program_id(0) == 0)
    def _():
        for i, first in enumerate(distances):
            for second in range(SIDE):
                start = (i * SIDE + second) * ROWS
                grads[start : start + ROWS] = grads_ref[chip_at(place_ref, first, second)]

    own, other = (jnp.concatenate([weights[i][...], weights[i + 1][...]], axis=1) for i in (0, 2))
    total = dot(grads[:, : 2 * HEAD], own, 1, 1)
    total += dot(grads[:, 2 * HEAD :], other, 1, 1)
    for i, out in enumerate(outs):
        out[...] = total[i * width : (i + 1) * width].astype(BF)


def weight_kernel(place_ref, grads_ref, *refs):
    blocks, (own_ref, other_ref, grads) = refs[:SIDE], refs[SIDE:]

    @pl.when(pl.program_id(0) == 0)
    def _():
        for i, second in enumerate(LINE):
            for first in range(SIDE):
                start = (i * SIDE + first) * ROWS
                grads[start : start + ROWS] = grads_ref[chip_at(place_ref, first, second)]

    rows = jnp.concatenate([ref[...] for ref in blocks], axis=0)
    total = dot(rows, grads[...], 0, 0).astype(BF)
    own_ref[...] = total[:, : 2 * HEAD]
    other_ref[...] = total[:, 2 * HEAD :]


def give_back_kernel(rank_ref, grads_ref, *outs):
    for d, out in zip(FAR_FIRST, outs):
        first = jnp.where(rank_ref[d][:1, :1] < 0.5, 1.0, 0.0).astype(BF)
        out[...] = jnp.where(first > 0.5, grads_ref[:SRC], grads_ref[SRC:])


def pick_kernel(place_ref, *refs):
    candidates, out_ref, sem = refs[:PLANES], refs[PLANES], refs[PLANES + 1]
    for d, ref in zip(FAR_FIRST, candidates):

        @pl.when(place_ref[3] == d)
        def _():
            copy = pltpu.make_async_copy(ref, out_ref, sem)
            copy.start()
            copy.wait()


def local(memory, lang_id, src_len, tgt_len, queries, key_weight, value_weight, grad_context):
    plane, y, x = lax.axis_index("lang"), lax.axis_index("y"), lax.axis_index("x")
    core = lax.axis_index("core")
    ahead = jnp.where(core == 0, lang_id[0] - plane, plane - lang_id[0])
    ahead = lax.rem(ahead + PLANES, PLANES)
    place = jnp.stack([plane, y, x, ahead, core]).astype(jnp.int32)

    with jax.named_scope("sentences_over_lang"):
        sentence = pl.pallas_call(
            label_kernel,
            out_shape=jax.ShapeDtypeStruct((SRC, WIDTH + HEAD), BF),
            in_specs=[VMEM] * 4,
            out_specs=VMEM,
            compiler_params=params(4),
        )(memory[0], *(number.reshape(1, 1) for number in (lang_id, src_len, tgt_len)))
        column = [sentence] + [shift_lang(sentence, d) for d in FAR_FIRST[1:]]

    with jax.named_scope("route"):
        routed, rank, lens = pl.pallas_call(
            route_kernel,
            out_shape=(
                jax.ShapeDtypeStruct((ROWS, WIDTH), BF),
                jax.ShapeDtypeStruct((PLANES, 8, HEAD), F32),
                jax.ShapeDtypeStruct((4, 8, HEAD), F32),
            ),
            in_specs=[SMEM] + [VMEM] * PLANES,
            out_specs=(VMEM,) * 3,
            compiler_params=params(16),
        )(place, *[column[FAR_FIRST.index(d)] for d in NEAR_FIRST])

    with jax.named_scope("weights_of_chip"):
        key_own, value_own, routed = lax.optimization_barrier(
            (key_weight[0], value_weight[0], routed)
        )
        weights = (key_own, value_own, exchange(key_own), exchange(value_own))

    with jax.named_scope("gather_rows"):
        line = pl.pallas_call(
            join_kernel,
            out_shape=jax.ShapeDtypeStruct((SIDE * ROWS, WIDTH), BF),
            in_specs=[ANY] * SIDE,
            out_specs=ANY,
            scratch_shapes=[pltpu.SemaphoreType.DMA((SIDE,))],
            compiler_params=params(1),
        )(routed, *[shift_plane(routed, 0, d) for d in LINE[1:]])
        blocks = [line] + [shift_plane(line, 1, d) for d in LINE[1:]]

    with jax.named_scope("project"):
        count = SIDE // 2
        scratch = [
            pltpu.VMEM((SIDE, count * SIDE * ROWS, WIDTH // SIDE), BF),
            pltpu.VMEM((SIDE, 2, WIDTH // SIDE, 2 * HEAD), BF),
            pltpu.VMEM((count * SIDE * ROWS, 4 * HEAD), F32),
            pltpu.SemaphoreType.DMA((SIDE, 4 + count)),
        ]
        block_at = dict(zip(LINE, blocks))
        early = pl.pallas_call(
            functools.partial(project_kernel, EARLY),
            out_shape=jax.ShapeDtypeStruct((count * SIDE * ROWS, 4 * HEAD), BF),
            in_specs=[SMEM] + [ANY] * (count + 4),
            out_specs=VMEM,
            scratch_shapes=scratch,
            compiler_params=params(24),
            cost_estimate=cost(count * SIDE * ROWS * WIDTH * 4 * HEAD, 6),
        )(place, *[block_at[d] for d in EARLY], *weights)
        projected = pl.pallas_call(
            functools.partial(project_rest_kernel, LATE),
            out_shape=jax.ShapeDtypeStruct((CHIPS, ROWS, 4 * HEAD), BF),
            in_specs=[SMEM, VMEM] + [ANY] * (count + 4),
            out_specs=VMEM,
            scratch_shapes=scratch + [pltpu.VMEM((count * SIDE * ROWS, 4 * HEAD), BF)],
            compiler_params=params(24),
            cost_estimate=cost(count * SIDE * ROWS * WIDTH * 4 * HEAD, 6),
        )(place, early, *[block_at[d] for d in LATE], *weights)

    with jax.named_scope("rows_to_slots"):
        slot_rows = lax.all_to_all(projected, PLANE, 0, 0, tiled=True)

    with jax.named_scope("attend"):
        groups = WIDTH // (GROUP * HEAD)
        wide = pl.BlockSpec((2, TGT, GROUP * HEAD), lambda g: (0, 0, g))
        narrow = pl.BlockSpec((GROUP // 2, ROWS, 4 * HEAD), lambda g: (g, 0, 0))
        tall = pl.BlockSpec((2, GROUP * SRC, TGT), lambda g: (0, g, 0))
        diagonal = [pltpu.VMEM((2, GROUP * SRC, GROUP * HEAD), BF)] * 2
        slot_grads, attention, grad_scores = pl.pallas_call(
            attend_kernel,
            grid=(groups,),
            out_shape=(jax.ShapeDtypeStruct((CHIPS, ROWS, 4 * HEAD), BF),)
            + (jax.ShapeDtypeStruct((2, groups * GROUP * SRC, TGT), BF),) * 2,
            in_specs=[SMEM, VMEM, wide, wide, narrow],
            out_specs=(narrow, tall, tall),
            scratch_shapes=diagonal,
            compiler_params=params(58),
            cost_estimate=cost(1 << 29, 6),
        )(place, lens, queries[0], grad_context[0], slot_rows)

    with jax.named_scope("grads_to_heads"):
        head_grads = lax.all_to_all(slot_grads, PLANE, 0, 0, tiled=True)

    with jax.named_scope("attend"):
        context, grad_queries = pl.pallas_call(
            outputs_kernel,
            grid=(groups,),
            out_shape=(jax.ShapeDtypeStruct((2, TGT, WIDTH), BF),) * 2,
            in_specs=[SMEM, VMEM, tall, tall, narrow],
            out_specs=(wide, wide),
            scratch_shapes=diagonal,
            compiler_params=params(32),
            cost_estimate=cost(1 << 30, 16),
        )(place, lens, attention, grad_scores, slot_rows)

    with jax.named_scope("sum_rows"):
        tile = WIDTH // SIDE
        terms = {}
        for distances in ((2, 1), (3, 0)):
            count = len(distances)
            found = pl.pallas_call(
                functools.partial(partial_kernel, distances),
                grid=(WIDTH // tile,),
                out_shape=(jax.ShapeDtypeStruct((SIDE * ROWS, WIDTH), BF),) * count,
                in_specs=[SMEM, VMEM] + [pl.BlockSpec((tile, HEAD), lambda t: (t, 0))] * 4,
                out_specs=(pl.BlockSpec((SIDE * ROWS, tile), lambda t: (0, t)),) * count,
                scratch_shapes=[pltpu.VMEM((count * SIDE * ROWS, 4 * HEAD), BF)],
                compiler_params=params(24),
                cost_estimate=cost(count * SIDE * ROWS * WIDTH * 4 * HEAD, 7),
            )(place, head_grads, *weights)
            terms.update(zip(distances, found))
        arrived = [terms[0]] + [shift_plane(terms[d], 0, -d) for d in LINE[1:]]
        arrived[1], context, grad_queries = lax.optimization_barrier(
            (arrived[1], context, grad_queries)
        )
        line = sum(term.astype(F32) for term in arrived).astype(BF)

    with jax.named_scope("weight_grads"):
        head_grads, _ = lax.optimization_barrier((head_grads, terms))
        tile = WIDTH // 8
        keep, send = pl.pallas_call(
            weight_kernel,
            grid=(WIDTH // tile,),
            out_shape=(jax.ShapeDtypeStruct((WIDTH, 2 * HEAD), BF),) * 2,
            in_specs=[SMEM, VMEM]
            + [pl.BlockSpec((SIDE * ROWS, tile), lambda t: (0, t))] * SIDE,
            out_specs=(pl.BlockSpec((tile, 2 * HEAD), lambda t: (t, 0)),) * 2,
            scratch_shapes=[pltpu.VMEM((CHIPS * ROWS, 4 * HEAD), BF)],
            compiler_params=params(32),
            cost_estimate=cost(CHIPS * ROWS * WIDTH * 4 * HEAD, 16),
        )(place, head_grads, *blocks)
        both = exchange(send)
        weight_grads = [
            (keep[:, cols].astype(F32) + both[:, cols].astype(F32)).astype(BF)
            for cols in (slice(0, HEAD), slice(HEAD, 2 * HEAD))
        ]

    with jax.named_scope("sum_rows"):
        pieces = {d: line[d * ROWS : (d + 1) * ROWS] for d in LINE}
        arrived = [pieces[0]] + [shift_plane(pieces[d], 1, -d) for d in LINE[1:]]
        arrived[1], weight_grads = lax.optimization_barrier((arrived[1], weight_grads))
        summed = sum(term.astype(F32) for term in arrived).astype(BF)

    with jax.named_scope("sentences_back"):
        sends = pl.pallas_call(
            give_back_kernel,
            out_shape=(jax.ShapeDtypeStruct((SRC, WIDTH), BF),) * PLANES,
            in_specs=[VMEM] * 2,
            out_specs=(VMEM,) * PLANES,
            compiler_params=params(16),
        )(rank, summed)
        candidates = [sends[0]] + [shift_lang(sends[i], -FAR_FIRST[i]) for i in range(1, PLANES)]
        grad_memory = pl.pallas_call(
            pick_kernel,
            out_shape=jax.ShapeDtypeStruct((SRC, WIDTH), BF),
            in_specs=[SMEM] + [ANY] * PLANES,
            out_specs=ANY,
            scratch_shapes=[pltpu.SemaphoreType.DMA],
            compiler_params=params(16),
        )(place, *candidates)

    return (
        context[None],
        grad_queries[None],
        grad_memory[None],
        weight_grads[0][None],
        weight_grads[1][None],
    )


def solution(mesh):
    planes = mesh.shape["lang"]
    grid = Mesh(mesh.devices.reshape(planes, SIDE, SIDE, 2), ("lang", "y", "x", "core"))
    shard = ("y", "x", "core")
    every = ("lang", "y", "x", "core")
    return jax.shard_map(
        local,
        mesh=grid,
        in_specs=(
            P(every, None, None),
            P(every),
            P(every),
            P(every),
            P("lang", shard, None, None),
            P("lang", None, shard),
            P("lang", None, shard),
            P("lang", shard, None, None),
        ),
        out_specs=(
            P("lang", shard, None, None),
            P("lang", shard, None, None),
            P(every, None, None),
            P("lang", None, shard),
            P("lang", None, shard),
        ),
        check_vma=False,
    )
```
